256 devices in a mesh: row: 16 (over y, z_lo, core), col: 16 (over x, z_hi).
Axes of the slice: x: 4, y: 4, z: 8 (z_hi: 4, z_lo: 2; z = z_hi * 2 + z_lo), core: 2. Of those that a mesh axis runs over, the one named last changes fastest.
Arguments:
- left_states: int32 [512, 8192], P(None, 'row'), may hold values from 0 to 3
- right_states: int32 [512, 4096], P(None, 'col'), may hold values from 0 to 3
- left_bias: float32 [4, 8192], P(None, 'row'), may hold values from -5 to 5
- right_bias: float32 [4, 4096], P(None, 'col'), may hold values from -5 to 5
- couplings: bfloat16 [4, 8192, 4, 4096], P(None, 'row', None, 'col'), may hold values from -0.09375 to 0.09375
Outputs:
- left_residual: bfloat16 [512, 4, 8192], P(None, None, 'row')
- right_residual: bfloat16 [512, 4, 4096], P(None, None, 'col')
- coupling_grad: bfloat16 [4, 8192, 4, 4096], P(None, 'row', None, 'col')
The draws below stay inside these ranges and needn't reach their ends.
All inputs are finite; a program needn't handle non-finite values.
Results may differ from the reference program's by a relative error of at most 0.011.
Values may be sent and summed in bfloat16 or wider, within the bound.
A program may use at most 128 MiB of HBM per device.

```python
import jax
import jax.numpy as jnp
from jax import lax

STATES = 4
NLEFT = 8192
NRIGHT = 4096
GEN = 512


def place_ends(result, key, least, largest):
    place = [jax.random.randint(jax.random.fold_in(key, axis), (), 0, length) for axis, length in enumerate(result.shape)]
    widest = result.shape.index(max(result.shape))
    neighbour = place[:widest] + [(place[widest] + 1) % result.shape[widest]] + place[widest + 1:]
    return result.at[tuple(place)].set(least).at[tuple(neighbour)].set(largest)


def block_levels(rng, shape, shards, smallest, top_value):
    gain = 1.0
    for axis_at, blocks in shards:
        heights = jax.random.uniform(jax.random.fold_in(jax.random.fold_in(rng, 6), axis_at), (blocks,), jnp.float32, smallest / len(shards), top_value / len(shards))
        gain = gain * jnp.repeat(jnp.exp(heights), shape[axis_at] // blocks).reshape((-1,) + (1,) * (len(shape) - 1 - axis_at))
    return gain


def gaussian(rng, dims, width, reach, pieces=(), kind=jnp.bfloat16):
    values = width * jax.random.normal(rng, dims, jnp.float32)
    if pieces:
        values = values * block_levels(rng, dims, pieces, -0.22, 0.18)
    return jnp.clip(values, -reach, reach).astype(kind)


def setup_inputs(seed: int = 0) -> dict:
    splits = jax.random.split(jax.random.key(seed), 6)
    return {
        "left_states": place_ends(jax.random.randint(splits[0], (GEN, NLEFT), 0, 4), jax.random.fold_in(splits[0], 1), 0, 3).astype(jnp.int32),
        "right_states": place_ends(jax.random.randint(splits[1], (GEN, NRIGHT), 0, 4), jax.random.fold_in(splits[1], 1), 0, 3).astype(jnp.int32),
        "left_bias": gaussian(splits[2], (STATES, NLEFT), 1.0, 5.0, ((1, 16),), jnp.float32),
        "right_bias": gaussian(splits[3], (STATES, NRIGHT), 1.0, 5.0, ((1, 16),), jnp.float32),
        "couplings": gaussian(splits[4], (STATES, NLEFT, STATES, NRIGHT), NRIGHT ** -0.5, 0.09375, ((1, 16), (3, 16))),
    }


def residual_of(fields, onehot):
    exps = jnp.exp(fields)
    probs = exps / jnp.sum(exps, axis=1, keepdims=True)
    return (onehot.astype(jnp.float32) - probs).astype(jnp.bfloat16)


def reference(left_states, right_states, left_bias, right_bias, couplings):
    state_ids = jnp.arange(STATES, dtype=jnp.int32)
    left_onehot = (left_states[:, None, :] == state_ids[None, :, None]).astype(jnp.bfloat16)
    right_onehot = (right_states[:, None, :] == state_ids[None, :, None]).astype(jnp.bfloat16)
    left_flat = left_onehot.reshape(GEN, STATES * NLEFT)
    right_flat = right_onehot.reshape(GEN, STATES * NRIGHT)
    matrix = couplings.reshape(STATES * NLEFT, STATES * NRIGHT)
    left_fields = jnp.dot(right_flat, matrix.T, preferred_element_type=jnp.float32).reshape(GEN, STATES, NLEFT) + left_bias[None]
    right_fields = jnp.dot(left_flat, matrix, preferred_element_type=jnp.float32).reshape(GEN, STATES, NRIGHT) + right_bias[None]
    left_residual = residual_of(left_fields, left_onehot)
    right_residual = residual_of(right_fields, right_onehot)
    stacked_left = jnp.concatenate([left_residual.reshape(GEN, STATES * NLEFT), left_flat], axis=0)
    stacked_right = jnp.concatenate([right_flat, right_residual.reshape(GEN, STATES * NRIGHT)], axis=0)
    blocks = jnp.transpose(stacked_left.reshape(2 * GEN, STATES, NLEFT), (1, 0, 2))

    def one_state(block):
        summed = jnp.dot(block.T, stacked_right, preferred_element_type=jnp.float32)
        return (-summed).astype(jnp.bfloat16)

    coupling_grad = lax.map(one_state, blocks).reshape(STATES, NLEFT, STATES, NRIGHT)
    return left_residual, right_residual, coupling_grad
```

```python
import jax
import jax.numpy as jnp
from jax import lax
from jax.experimental import pallas as pl
from jax.experimental.pallas import tpu as pltpu
from jax.sharding import PartitionSpec as P

MESH = pl.DeviceIdType.MESH
BF = jnp.bfloat16
F32 = jnp.float32
PIECES = 4
VMEM_LIMIT = 56 * 1024 * 1024


def permutation(rows, inner):
    outer = rows // inner
    at = lax.broadcasted_iota(jnp.int32, (rows, rows), 0)
    of = lax.broadcasted_iota(jnp.int32, (rows, rows), 1)
    want = lax.rem(at, outer) * inner + lax.div(at, outer)
    return jnp.where(of == want, 1.0, 0.0).astype(BF)


def onehot(states, value):
    return jnp.where(states == value, 1.0, 0.0).astype(BF)


def softmax_residual(diffs, states):
    top = jnp.maximum(jnp.maximum(diffs[0], diffs[1]), jnp.maximum(diffs[2], 0.0))
    exps = [jnp.exp(d - top) for d in diffs]
    inverse = 1.0 / (exps[0] + exps[1] + exps[2] + jnp.exp(-top))
    return [
        (jnp.where(states == a, 1.0, 0.0) - exps[a] * inverse).astype(BF) for a in range(3)
    ]


def exchange_kernel(
    left_ref, right_ref, lbias_ref, rbias_ref, coup_ref,
    rg_out, rr_out,
    raw, flat, perm, rt, loh, slt, bt,
    lp, xa, xb, zp, za, zb, rg,
    cs, cr, own, yp, ya, yb, tz, zs, zr, rr,
    in_sem, out_sem, lsend, lrecv, rsend, rrecv,
):
    row = lax.axis_index("row")
    col = lax.axis_index("col")
    core = lax.rem(row, 2)
    zl = lax.rem(lax.div(row, 2), 2)
    y = lax.div(row, 4)
    x = lax.div(col, 4)
    z = lax.rem(col, 4)

    def at_x(v):
        return {"row": row, "col": lax.rem(v, 4) * 4 + z}

    def at_z(v):
        return {"row": row, "col": x * 4 + lax.rem(v, 4)}

    def at_y(v):
        return {"row": lax.rem(v, 4) * 4 + zl * 2 + core, "col": col}

    x_next, x_prev, z_next, z_prev = at_x(x + 1), at_x(x + 3), at_z(z + 1), at_z(z + 3)
    y_next, y_prev = at_y(y + 1), at_y(y + 3)
    core_peer = {"row": y * 4 + zl * 2 + 1 - core, "col": col}
    zl_peer = {"row": y * 4 + (1 - zl) * 2 + core, "col": col}
    peers = (x_next, x_prev, z_next, z_prev, y_next, y_prev, core_peer, zl_peer)

    barrier = pltpu.get_barrier_semaphore()
    for peer in peers:
        pl.semaphore_signal(barrier, inc=1, device_id=peer, device_id_type=MESH)

    loads = []
    for p in range(PIECES):
        rows = pl.ds(p * 1024, 1024)
        load = pltpu.make_async_copy(coup_ref.at[:, rows, :], raw.at[:, rows, :], in_sem.at[p])
        load.start()
        loads.append(load)

    sent = []

    def send(src, dst, sems, slot, peer):
        copy = pltpu.make_async_remote_copy(
            src_ref=src, dst_ref=dst, send_sem=sems[0].at[slot], recv_sem=sems[1].at[slot],
            device_id=peer, device_id_type=MESH,
        )
        copy.start()
        sent.append(copy)
        return copy

    lsems = (lsend, lrecv)
    rsems = (rsend, rrecv)

    perm[...] = permutation(256, 8)
    right_t = right_ref[...].T
    for b in range(4):
        rt[pl.ds(b * 256, 256), :] = onehot(right_t, b)

    live = {}

    def s0(p):
        loads[p].wait()
        for a in range(4):
            for h in range(2):
                pair = [
                    raw[a, pl.ds(p * 1024 + (2 * h + k) * 256, 256), :] for k in range(2)
                ]
                turned = jnp.dot(
                    perm[...], jnp.concatenate(pair, axis=1), preferred_element_type=F32
                ).astype(BF)
                for k in range(2):
                    for jt in range(2):
                        for b in range(4):
                            flat[
                                pl.ds(a * 512 + p * 128 + (2 * h + k) * 32, 32),
                                pl.ds(b * 256 + jt * 128, 128),
                            ] = turned[(jt * 4 + b) * 32:(jt * 4 + b + 1) * 32, k * 128:(k + 1) * 128]
        lhs = jnp.concatenate([flat[pl.ds(a * 512 + p * 128, 128), :] for a in range(4)], axis=0)
        fields = jnp.dot(lhs, rt[...], preferred_element_type=F32)
        for a in range(3):
            diff = (fields[a * 128:(a + 1) * 128] - fields[384:512]).astype(BF)
            for xc in range(4):
                for zc in range(4):
                    lp[p, xc, zc, a] = diff[zc * 32:(zc + 1) * 32, xc * 128:(xc + 1) * 128]

    def s0_send(p):
        opp, nxt, prv = lax.rem(x + 2, 4), lax.rem(x + 1, 4), lax.rem(x + 3, 4)
        lo, hi = pl.ds(0, 2), pl.ds(2, 2)
        live[p, 0] = send(lp.at[p, opp, lo], xa.at[p, 0], lsems, p * 20 + 0, x_next)
        live[p, 1] = send(lp.at[p, opp, hi], xa.at[p, 1], lsems, p * 20 + 1, x_prev)
        live[p, 2] = send(lp.at[p, nxt, hi], xb.at[p, 0, hi], lsems, p * 20 + 2, x_next)
        live[p, 3] = send(lp.at[p, prv, lo], xb.at[p, 1, lo], lsems, p * 20 + 3, x_prev)

    def s1(p):
        nxt, prv = lax.rem(x + 1, 4), lax.rem(x + 3, 4)
        lo, hi = pl.ds(0, 2), pl.ds(2, 2)
        live[p, 0].wait_recv()
        lp[p, nxt, lo] = (lp[p, nxt, lo].astype(F32) + xa[p, 0].astype(F32)).astype(BF)
        live[p, 4] = send(lp.at[p, nxt, lo], xb.at[p, 0, lo], lsems, p * 20 + 4, x_next)
        live[p, 1].wait_recv()
        lp[p, prv, hi] = (lp[p, prv, hi].astype(F32) + xa[p, 1].astype(F32)).astype(BF)
        live[p, 5] = send(lp.at[p, prv, hi], xb.at[p, 1, hi], lsems, p * 20 + 5, x_prev)

    def s2(p):
        for m in (2, 3, 4, 5):
            live[p, m].wait_recv()
        zp[p] = (
            lp[p, x].astype(F32) + xb[p, 0].astype(F32) + xb[p, 1].astype(F32)
        ).astype(BF)
        opp, nxt, prv = lax.rem(z + 2, 4), lax.rem(z + 1, 4), lax.rem(z + 3, 4)
        lo, hi = pl.ds(0, 16), pl.ds(16, 16)
        live[p, 6] = send(zp.at[p, opp, :, lo], za.at[p, 0], lsems, p * 20 + 6, z_next)
        live[p, 7] = send(zp.at[p, opp, :, hi], za.at[p, 1], lsems, p * 20 + 7, z_prev)
        live[p, 8] = send(zp.at[p, nxt, :, hi], zb.at[p, 0, :, hi], lsems, p * 20 + 8, z_next)
        live[p, 9] = send(zp.at[p, prv, :, lo], zb.at[p, 1, :, lo], lsems, p * 20 + 9, z_prev)

    def s3(p):
        nxt, prv = lax.rem(z + 1, 4), lax.rem(z + 3, 4)
        lo, hi = pl.ds(0, 16), pl.ds(16, 16)
        live[p, 6].wait_recv()
        zp[p, nxt, :, lo] = (zp[p, nxt, :, lo].astype(F32) + za[p, 0].astype(F32)).astype(BF)
        live[p, 10] = send(zp.at[p, nxt, :, lo], zb.at[p, 0, :, lo], lsems, p * 20 + 10, z_next)
        live[p, 7].wait_recv()
        zp[p, prv, :, hi] = (zp[p, prv, :, hi].astype(F32) + za[p, 1].astype(F32)).astype(BF)
        live[p, 11] = send(zp.at[p, prv, :, hi], zb.at[p, 1, :, hi], lsems, p * 20 + 11, z_prev)

    def s4(p):
        for m in (8, 9, 10, 11):
            live[p, m].wait_recv()
        total = zp[p, z].astype(F32) + zb[p, 0].astype(F32) + zb[p, 1].astype(F32)
        rows = pl.ds(pl.multiple_of(p * 128 + z * 32, 32), 32)
        diffs = [total[a] + bt[a, rows, :] for a in range(3)]
        result = softmax_residual(diffs, slt[x, rows, :])
        for a in range(3):
            rg[p, x, z, a] = result[a]
        block = rg.at[p, x, z]
        live[p, 12] = send(block, block, lsems, p * 20 + 12, z_next)
        live[p, 13] = send(block, block, lsems, p * 20 + 13, z_prev)

    def s5(p):
        nxt, prv = lax.rem(z + 1, 4), lax.rem(z + 3, 4)
        live[p, 12].wait_recv()
        block = rg.at[p, x, prv, :, pl.ds(0, 16)]
        live[p, 14] = send(block, block, lsems, p * 20 + 14, z_next)
        live[p, 13].wait_recv()
        block = rg.at[p, x, nxt, :, pl.ds(16, 16)]
        live[p, 15] = send(block, block, lsems, p * 20 + 15, z_prev)

    def s6(p):
        live[p, 14].wait_recv()
        live[p, 15].wait_recv()
        block = rg.at[p, x]
        live[p, 16] = send(block, block, lsems, p * 20 + 16, x_next)
        live[p, 17] = send(block, block, lsems, p * 20 + 17, x_prev)

    def s7(p):
        nxt, prv = lax.rem(x + 1, 4), lax.rem(x + 3, 4)
        live[p, 16].wait_recv()
        block = rg.at[p, prv, pl.ds(0, 2)]
        live[p, 18] = send(block, block, lsems, p * 20 + 18, x_next)
        live[p, 17].wait_recv()
        block = rg.at[p, nxt, pl.ds(2, 2)]
        live[p, 19] = send(block, block, lsems, p * 20 + 19, x_prev)

    finals = []

    def s8(p):
        live[p, 18].wait_recv()
        live[p, 19].wait_recv()
        copy = pltpu.make_async_copy(rg.at[p], rg_out.at[p], out_sem.at[p])
        copy.start()
        finals.append(copy)

    def right_diffs(half):
        lhs = loh[pl.ds(pl.multiple_of(half * 256, 256), 256), :]
        fields = jnp.dot(lhs, flat[...], preferred_element_type=F32)
        return [fields[:, b * 256:(b + 1) * 256] - fields[:, 768:1024] for b in range(3)]

    def r0():
        for b, diff in enumerate(right_diffs(1 - core)):
            cs[:, pl.ds(b * 256, 256)] = diff.astype(BF)
        live["c"] = send(cs, cr, rsems, 0, core_peer)
        for b, diff in enumerate(right_diffs(core)):
            own[:, pl.ds(b * 256, 256)] = diff

    def r1():
        live["c"].wait_recv()
        for c in range(4):
            rows = pl.ds(c * 64, 64)
            yp[c] = (own[rows, :] + cr[rows, :].astype(F32)).astype(BF)
        opp, nxt, prv = lax.rem(y + 2, 4), lax.rem(y + 1, 4), lax.rem(y + 3, 4)
        lo, hi = pl.ds(0, 32), pl.ds(32, 32)
        live["y0"] = send(yp.at[opp, lo], ya.at[0], rsems, 1, y_next)
        live["y1"] = send(yp.at[opp, hi], ya.at[1], rsems, 2, y_prev)
        live["y2"] = send(yp.at[nxt, hi], yb.at[0, hi], rsems, 3, y_next)
        live["y3"] = send(yp.at[prv, lo], yb.at[1, lo], rsems, 4, y_prev)

    def r2():
        nxt, prv = lax.rem(y + 1, 4), lax.rem(y + 3, 4)
        lo, hi = pl.ds(0, 32), pl.ds(32, 32)
        live["y0"].wait_recv()
        yp[nxt, lo] = (yp[nxt, lo].astype(F32) + ya[0].astype(F32)).astype(BF)
        live["y4"] = send(yp.at[nxt, lo], yb.at[0, lo], rsems, 5, y_next)
        live["y1"].wait_recv()
        yp[prv, hi] = (yp[prv, hi].astype(F32) + ya[1].astype(F32)).astype(BF)
        live["y5"] = send(yp.at[prv, hi], yb.at[1, hi], rsems, 6, y_prev)

    def r3():
        for name in ("y2", "y3", "y4", "y5"):
            live[name].wait_recv()
        total = yp[y].astype(F32) + yb[0].astype(F32) + yb[1].astype(F32)
        tz[0] = total[:32]
        tz[1] = total[32:]
        zs[...] = tz[1 - zl].astype(BF)
        live["z0"] = send(zs, zr, rsems, 7, zl_peer)

    def rows_at(core_at, y_at, zl_at, count):
        return pl.ds(pl.multiple_of(core_at * 256 + y_at * 64 + zl_at * 32, 32), count)

    def r4():
        live["z0"].wait_recv()
        total = tz[zl] + zr[...].astype(F32)
        rows = rows_at(core, y, zl, 32)
        base = rbias_ref[pl.ds(3, 1), :]
        diffs = [
            total[:, b * 256:(b + 1) * 256] + (rbias_ref[pl.ds(b, 1), :] - base) for b in range(3)
        ]
        for b, part in enumerate(softmax_residual(diffs, right_ref[rows, :])):
            rr[rows, pl.ds(b * 256, 256)] = part
        block = rr.at[rows, :]
        live["z1"] = send(block, block, rsems, 8, zl_peer)

    def r5():
        live["z1"].wait_recv()
        block = rr.at[rows_at(core, y, 0, 64), :]
        live["y6"] = send(block, block, rsems, 9, y_next)
        live["y7"] = send(block, block, rsems, 10, y_prev)

    def r6():
        nxt, prv = lax.rem(y + 1, 4), lax.rem(y + 3, 4)
        live["y6"].wait_recv()
        block = rr.at[rows_at(core, prv, 0, 32), :]
        live["y8"] = send(block, block, rsems, 11, y_next)
        live["y7"].wait_recv()
        block = rr.at[rows_at(core, nxt, 1, 32), :]
        live["y9"] = send(block, block, rsems, 12, y_prev)

    def r7():
        live["y8"].wait_recv()
        live["y9"].wait_recv()
        block = rr.at[rows_at(core, 0, 0, 256), :]
        live["c1"] = send(block, block, rsems, 13, core_peer)

    def r8():
        live["c1"].wait_recv()
        copy = pltpu.make_async_copy(rr, rr_out, out_sem.at[PIECES])
        copy.start()
        finals.append(copy)

    def left_tables():
        left_t = left_ref[...].T
        for xc in range(4):
            slt[xc] = left_t[:, xc * 128:(xc + 1) * 128]
        base = lbias_ref[pl.ds(3, 1), :]
        for a in range(3):
            diff = lbias_ref[pl.ds(a, 1), :] - base
            for p in range(PIECES):
                part = jnp.broadcast_to(diff[:, p * 128:(p + 1) * 128], (128, 128))
                bt[a, pl.ds(p * 128, 128), :] = part.T

    def left_onehots():
        states = left_ref[...]
        for a in range(4):
            loh[:, pl.ds(a * 512, 512)] = onehot(states, a)

    s0(0)
    pl.semaphore_wait(barrier, len(peers))
    s0_send(0)
    left_stages = (None, s1, s2, s3, s4, s5, s6, s7, s8)
    right_stages = (r0, r1, r2, r3, r4, r5, r6, r7, r8)
    for tick in range(1, PIECES + 9):
        if tick < PIECES:
            s0(tick)
            s0_send(tick)
        if tick == 1:
            left_tables()
        if tick == 2:
            left_onehots()
        for p in range(PIECES):
            if 0 < tick - p < 9:
                left_stages[tick - p](p)
        if 0 <= tick - PIECES + 1 < 9:
            right_stages[tick - PIECES + 1]()
    for copy in sent:
        copy.wait_send()
    for copy in finals:
        copy.wait()


def exchange(left_states, right_states, left_bias, right_bias, couplings):
    vmem = pl.BlockSpec(memory_space=pltpu.VMEM)
    hbm = pl.BlockSpec(memory_space=pl.ANY)
    n = PIECES
    return pl.pallas_call(
        exchange_kernel,
        out_shape=(
            jax.ShapeDtypeStruct((n, 4, 4, 3, 32, 128), BF),
            jax.ShapeDtypeStruct((512, 768), BF),
        ),
        in_specs=[vmem] * 4 + [hbm],
        out_specs=(hbm, hbm),
        scratch_shapes=[
            pltpu.VMEM((4, 4096, 128), BF),
            pltpu.VMEM((2048, 1024), BF),
            pltpu.VMEM((256, 256), BF),
            pltpu.VMEM((1024, 512), BF),
            pltpu.VMEM((512, 2048), BF),
            pltpu.VMEM((4, 512, 128), jnp.int32),
            pltpu.VMEM((3, 512, 128), F32),
            pltpu.VMEM((n, 4, 4, 3, 32, 128), BF),
            pltpu.VMEM((n, 2, 2, 3, 32, 128), BF),
            pltpu.VMEM((n, 2, 4, 3, 32, 128), BF),
            pltpu.VMEM((n, 4, 3, 32, 128), BF),
            pltpu.VMEM((n, 2, 3, 16, 128), BF),
            pltpu.VMEM((n, 2, 3, 32, 128), BF),
            pltpu.VMEM((n, 4, 4, 3, 32, 128), BF),
            pltpu.VMEM((256, 768), BF),
            pltpu.VMEM((256, 768), BF),
            pltpu.VMEM((256, 768), F32),
            pltpu.VMEM((4, 64, 768), BF),
            pltpu.VMEM((2, 32, 768), BF),
            pltpu.VMEM((2, 64, 768), BF),
            pltpu.VMEM((2, 32, 768), F32),
            pltpu.VMEM((32, 768), BF),
            pltpu.VMEM((32, 768), BF),
            pltpu.VMEM((512, 768), BF),
            pltpu.SemaphoreType.DMA((n,)),
            pltpu.SemaphoreType.DMA((n + 1,)),
            pltpu.SemaphoreType.DMA((n * 20,)),
            pltpu.SemaphoreType.DMA((n * 20,)),
            pltpu.SemaphoreType.DMA((14,)),
            pltpu.SemaphoreType.DMA((14,)),
        ],
        compiler_params=pltpu.CompilerParams(
            collective_id=0, has_side_effects=True, vmem_limit_bytes=VMEM_LIMIT
        ),
        name="exchange",
    )(left_states, right_states, left_bias, right_bias, couplings)


def gradient_kernel(left_ref, right_ref, rg_ref, rr_ref, lres_ref, rres_ref, grad_ref, rhs, perm, perm16):
    g = pl.program_id(0)

    @pl.when(g == 0)
    def _():
        perm[...] = permutation(256, 32)
        perm16[...] = permutation(256, 16)
        states = right_ref[...]
        total = jnp.zeros((512, 256), F32)
        for b in range(4):
            rhs[pl.ds(0, 512), pl.ds(b * 256, 256)] = -onehot(states, b)
        for b in range(3):
            part = rr_ref[:, pl.ds(b * 256, 256)]
            rhs[pl.ds(512, 512), pl.ds(b * 256, 256)] = -part
            total += part.astype(F32)
        rhs[pl.ds(512, 512), pl.ds(768, 256)] = total.astype(BF)

    rows = pl.ds(pl.multiple_of(512 + g * 128, 128), 128)
    part = -rhs[rows, :]
    for h in range(2):
        stack = jnp.concatenate(
            [
                jnp.concatenate(
                    [
                        part[(2 * h + k) * 32:(2 * h + k + 1) * 32, b * 256 + jt * 128:b * 256 + (jt + 1) * 128]
                        for jt in range(2) for b in range(4)
                    ],
                    axis=0,
                )
                for k in range(2)
            ],
            axis=1,
        )
        turned = jnp.dot(perm[...], stack, preferred_element_type=F32).astype(BF)
        for k in range(2):
            rres_ref[pl.ds((2 * h + k) * 256, 256), :] = turned[:, k * 128:(k + 1) * 128]

    natural = []
    for p in range(PIECES):
        blocks = [rg_ref[p, g, :, a].reshape(128, 128).astype(F32) for a in range(3)]
        blocks.append(-(blocks[0] + blocks[1] + blocks[2]))
        natural.extend([block.T.astype(BF) for block in blocks])
    for h in range(4):
        stack = jnp.concatenate(
            [
                jnp.concatenate([block[(2 * h + k) * 16:(2 * h + k + 1) * 16] for block in natural], axis=0)
                for k in range(2)
            ],
            axis=1,
        )
        turned = jnp.dot(perm16[...], stack, preferred_element_type=F32).astype(BF)
        for k in range(2):
            lres_ref[pl.ds((2 * h + k) * 256, 256), :] = turned[:, k * 128:(k + 1) * 128]

    left_t = left_ref[...].T
    parts = [
        jnp.concatenate([rg_ref[g, xc, :, a].reshape(128, 128) for xc in range(4)], axis=1)
        for a in range(3)
    ]
    last = -(parts[0].astype(F32) + parts[1].astype(F32) + parts[2].astype(F32))
    parts.append(last.astype(BF))
    lhs = jnp.concatenate(
        [jnp.concatenate([parts[a], onehot(left_t, a)], axis=1) for a in range(4)], axis=0
    )
    summed = jnp.dot(lhs, rhs[...], preferred_element_type=F32).astype(BF)
    for a in range(4):
        for h in range(2):
            stack = jnp.concatenate(
                [
                    jnp.concatenate(
                        [
                            summed[
                                a * 128 + (2 * h + k) * 32:a * 128 + (2 * h + k + 1) * 32,
                                b * 256 + jt * 128:b * 256 + (jt + 1) * 128,
                            ]
                            for jt in range(2) for b in range(4)
                        ],
                        axis=0,
                    )
                    for k in range(2)
                ],
                axis=1,
            )
            turned = jnp.dot(perm[...], stack, preferred_element_type=F32).astype(BF)
            for k in range(2):
                grad_ref[a, pl.ds((2 * h + k) * 256, 256), :] = turned[:, k * 128:(k + 1) * 128]


def gradient(left_states, right_states, rg, rr):
    whole = pl.BlockSpec(memory_space=pltpu.VMEM)
    return pl.pallas_call(
        gradient_kernel,
        grid=(PIECES,),
        out_shape=(
            jax.ShapeDtypeStruct((8192, 128), BF),
            jax.ShapeDtypeStruct((4096, 128), BF),
            jax.ShapeDtypeStruct((4, 4096, 128), BF),
        ),
        in_specs=[pl.BlockSpec((512, 128), lambda g: (0, g)), whole, whole, whole],
        out_specs=(
            pl.BlockSpec((2048, 128), lambda g: (g, 0)),
            pl.BlockSpec((1024, 128), lambda g: (g, 0)),
            pl.BlockSpec((4, 1024, 128), lambda g: (0, g, 0)),
        ),
        scratch_shapes=[
            pltpu.VMEM((1024, 1024), BF),
            pltpu.VMEM((256, 256), BF),
            pltpu.VMEM((256, 256), BF),
        ],
        compiler_params=pltpu.CompilerParams(vmem_limit_bytes=VMEM_LIMIT),
        name="gradient",
    )(left_states, right_states, rg, rr)


def body(left_states, right_states, left_bias, right_bias, couplings):
    view = couplings.reshape(4, 512, 4, 2, 128).transpose(0, 1, 3, 2, 4).reshape(4, 4096, 128)
    rg, rr = exchange(left_states, right_states, left_bias, right_bias, view)
    left, right, grad = gradient(left_states, right_states, rg, rr)
    left_residual = left.reshape(512, 4, 4, 128).transpose(0, 2, 1, 3).reshape(512, 4, 512)
    right_residual = right.reshape(512, 2, 4, 128).transpose(0, 2, 1, 3).reshape(512, 4, 256)
    coupling_grad = grad.reshape(4, 512, 2, 4, 128).transpose(0, 1, 3, 2, 4).reshape(4, 512, 4, 256)
    return left_residual, right_residual, coupling_grad


def solution(mesh):
    in_specs = (
        P(None, "row"),
        P(None, "col"),
        P(None, "row"),
        P(None, "col"),
        P(None, "row", None, "col"),
    )
    out_specs = (P(None, None, "row"), P(None, None, "col"), P(None, "row", None, "col"))
    return jax.shard_map(body, mesh=mesh, in_specs=in_specs, out_specs=out_specs, check_vma=False)
```

```python
import jax
import jax.numpy as jnp
from jax import lax
from jax.experimental import pallas as pl
from jax.experimental.pallas import tpu as pltpu
from jax.sharding import PartitionSpec as P

MESH = pl.DeviceIdType.MESH
BF = jnp.bfloat16
F32 = jnp.float32
PIECES = 4
DIRECT_SCATTER = (0,)
DIRECT_GATHER = (3,)
EXCHANGE_VMEM = 40 * 1024 * 1024
FINISH_VMEM = 24 * 1024 * 1024


def permutation(inner_bits):
    outer_bits = 8 - inner_bits
    at = lax.broadcasted_iota(jnp.int32, (256, 256), 0)
    of = lax.broadcasted_iota(jnp.int32, (256, 256), 1)
    want = ((at & ((1 << outer_bits) - 1)) << inner_bits) + (at >> outer_bits)
    return jnp.where(of == want, 1.0, 0.0).astype(BF)


def side_by_side(blocks):
    return jnp.concatenate([jnp.concatenate(rows, axis=0) for rows in blocks], axis=1)


def spread_states(perm, values, store):
    for h in range(values.shape[0] // 64):
        stack = side_by_side(
            [
                [
                    values[(2 * h + k) * 32:(2 * h + k + 1) * 32, b * 256 + jt * 128:b * 256 + (jt + 1) * 128]
                    for jt in range(2) for b in range(4)
                ]
                for k in range(2)
            ]
        )
        turned = jnp.dot(perm, stack, preferred_element_type=F32).astype(BF)
        for k in range(2):
            store(2 * h + k, turned[:, k * 128:(k + 1) * 128])


def four_states(parts):
    last = -(parts[0].astype(F32) + parts[1].astype(F32) + parts[2].astype(F32))
    return list(parts) + [last.astype(BF)]


def piece_rows(rg):
    return four_states(
        [
            jnp.concatenate([rg[xc, :, a].reshape(128, 128) for xc in range(4)], axis=1)
            for a in range(3)
        ]
    )


def onehot(states, value):
    return jnp.where(states == value, 1.0, 0.0).astype(BF)


def softmax_residual(diffs, states):
    top = jnp.maximum(jnp.maximum(diffs[0], diffs[1]), jnp.maximum(diffs[2], 0.0))
    exps = [jnp.exp(d - top) for d in diffs]
    inverse = 1.0 / (exps[0] + exps[1] + exps[2] + jnp.exp(-top))
    return [
        (jnp.where(states == a, 1.0, 0.0) - exps[a] * inverse).astype(BF) for a in range(3)
    ]


def exchange_kernel(
    left_in, right_in, lbias_in, rbias_in, coup_ref,
    grad_out, nat_out, rres_out, rhs_out, rg_out, lht_out,
    left_ref, right_ref, lbias_ref, rbias_ref, raw, flat, perm, spread, grads, nat, rres, rhs, lht, rt, loh, slt, bt,
    lp, xa, xb, zp, zb, rg,
    cs, cr, own, yp, yb, rr,
    in_sem, out_sem, lsend, lrecv, rsend, rrecv,
):
    row = lax.axis_index("row")
    col = lax.axis_index("col")
    core = lax.rem(row, 2)
    zl = lax.rem(lax.div(row, 2), 2)
    y = lax.div(row, 4)
    x = lax.div(col, 4)
    z = lax.rem(col, 4)

    def at_x(d):
        return {"row": row, "col": lax.rem(x + d, 4) * 4 + z}

    def at_z(d):
        return {"row": row, "col": x * 4 + lax.rem(z + d, 4)}

    def at_yz(d):
        return {"row": lax.rem(y + d // 2, 4) * 4 + lax.rem(zl + d % 2, 2) * 2 + core, "col": col}

    x_next, x_prev = at_x(1), at_x(3)
    core_peer = {"row": y * 4 + zl * 2 + 1 - core, "col": col}
    peers = (
        [at_x(d) for d in (1, 2, 3)] + [at_z(d) for d in (1, 2, 3)]
        + [at_yz(d) for d in range(1, 8)] + [core_peer]
    )

    barrier = pltpu.get_barrier_semaphore()
    for peer in peers:
        pl.semaphore_signal(barrier, inc=1, device_id=peer, device_id_type=MESH)

    loads = {}

    def load(key, src, dst):
        copy = pltpu.make_async_copy(src, dst, in_sem.at[len(loads)])
        copy.start()
        loads[key] = copy

    load("right", right_in, right_ref)
    for p in range(PIECES):
        rows = pl.ds(p * 1024, 1024)
        load(p, coup_ref.at[:, rows, :], raw.at[:, rows, :])
        if p == 0:
            load("left", left_in, left_ref)
            load("lbias", lbias_in, lbias_ref)
            load("rbias", rbias_in, rbias_ref)

    sent = []

    def send(src, dst, sems, slot, peer):
        copy = pltpu.make_async_remote_copy(
            src_ref=src, dst_ref=dst, send_sem=sems[0].at[slot], recv_sem=sems[1].at[slot],
            device_id=peer, device_id_type=MESH,
        )
        copy.start()
        sent.append(copy)
        return copy

    lsems = (lsend, lrecv)
    rsems = (rsend, rrecv)

    perm[...] = permutation(3)
    spread[...] = permutation(5)
    loads["right"].wait()
    right_t = right_ref[...].T
    for b in range(4):
        rt[pl.ds(b * 256, 256), :] = onehot(right_t, b)

    live = {}

    def left_fields(p):
        loads[p].wait()
        for a in range(4):
            for h in range(2):
                pair = [
                    raw[a, pl.ds(p * 1024 + (2 * h + k) * 256, 256), :] for k in range(2)
                ]
                turned = jnp.dot(
                    perm[...], jnp.concatenate(pair, axis=1), preferred_element_type=F32
                ).astype(BF)
                for k in range(2):
                    for jt in range(2):
                        for b in range(4):
                            flat[
                                pl.ds(a * 512 + p * 128 + (2 * h + k) * 32, 32),
                                pl.ds(b * 256 + jt * 128, 128),
                            ] = turned[(jt * 4 + b) * 32:(jt * 4 + b + 1) * 32, k * 128:(k + 1) * 128]
        lhs = jnp.concatenate([flat[pl.ds(a * 512 + p * 128, 128), :] for a in range(4)], axis=0)
        fields = jnp.dot(lhs, rt[...], preferred_element_type=F32)
        for a in range(3):
            diff = (fields[a * 128:(a + 1) * 128] - fields[384:512]).astype(BF)
            for xc in range(4):
                for zc in range(4):
                    lp[p, xc, zc, a] = diff[zc * 32:(zc + 1) * 32, xc * 128:(xc + 1) * 128]

    def x_scatter(p):
        if p in DIRECT_SCATTER:
            for d in (2, 1, 3):
                live[p, d] = send(lp.at[p, lax.rem(x + d, 4)], xb.at[p, d - 1], lsems, p * 16 + d, at_x(d))
            return
        opp, nxt, prv = lax.rem(x + 2, 4), lax.rem(x + 1, 4), lax.rem(x + 3, 4)
        lo, hi = pl.ds(0, 2), pl.ds(2, 2)
        live[p, 0] = send(lp.at[p, opp, lo], xa.at[p, 0], lsems, p * 16 + 0, x_next)
        live[p, 1] = send(lp.at[p, opp, hi], xa.at[p, 1], lsems, p * 16 + 1, x_prev)
        live[p, 2] = send(lp.at[p, nxt, hi], xb.at[p, 0, hi], lsems, p * 16 + 2, x_next)
        live[p, 3] = send(lp.at[p, prv, lo], xb.at[p, 1, lo], lsems, p * 16 + 3, x_prev)

    def x_relay(p):
        nxt, prv = lax.rem(x + 1, 4), lax.rem(x + 3, 4)
        lo, hi = pl.ds(0, 2), pl.ds(2, 2)
        live[p, 0].wait_recv()
        lp[p, nxt, lo] = (lp[p, nxt, lo].astype(F32) + xa[p, 0].astype(F32)).astype(BF)
        live[p, 4] = send(lp.at[p, nxt, lo], xb.at[p, 0, lo], lsems, p * 16 + 4, x_next)
        live[p, 1].wait_recv()
        lp[p, prv, hi] = (lp[p, prv, hi].astype(F32) + xa[p, 1].astype(F32)).astype(BF)
        live[p, 5] = send(lp.at[p, prv, hi], xb.at[p, 1, hi], lsems, p * 16 + 5, x_prev)

    def z_scatter(p):
        direct = p in DIRECT_SCATTER
        for m in (1, 2, 3) if direct else (2, 3, 4, 5):
            live[p, m].wait_recv()
        total = lp[p, x].astype(F32) + xb[p, 0].astype(F32) + xb[p, 1].astype(F32)
        if direct:
            total = total + xb[p, 2].astype(F32)
        zp[p] = total.astype(BF)
        for d in (2, 1, 3):
            live[p, 5 + d] = send(zp.at[p, lax.rem(z + d, 4)], zb.at[p, d - 1], lsems, p * 16 + 5 + d, at_z(d))

    def z_gather(p):
        for m in (6, 7, 8):
            live[p, m].wait_recv()
        total = zp[p, z].astype(F32)
        for k in range(3):
            total = total + zb[p, k].astype(F32)
        rows = pl.ds(pl.multiple_of(p * 128 + z * 32, 32), 32)
        diffs = [total[a] + bt[a, rows, :] for a in range(3)]
        result = softmax_residual(diffs, slt[x, rows, :])
        for a in range(3):
            rg[p, x, z, a] = result[a]
        block = rg.at[p, x, z]
        for d in (2, 1, 3):
            live[p, 8 + d] = send(block, block, lsems, p * 16 + 8 + d, at_z(d))

    def x_gather(p):
        for m in (9, 10, 11):
            live[p, m].wait_recv()
        block = rg.at[p, x]
        for d in (2, 1, 3) if p in DIRECT_GATHER else (1, 3):
            live[p, 11 + d] = send(block, block, lsems, p * 16 + 11 + d, at_x(d))

    def x_forward(p):
        nxt, prv = lax.rem(x + 1, 4), lax.rem(x + 3, 4)
        live[p, 12].wait_recv()
        block = rg.at[p, prv, pl.ds(0, 2)]
        live[p, 13] = send(block, block, lsems, p * 16 + 13, x_next)
        live[p, 14].wait_recv()
        block = rg.at[p, nxt, pl.ds(2, 2)]
        live[p, 15] = send(block, block, lsems, p * 16 + 15, x_prev)

    finals = []

    def keep(src, dst):
        copy = pltpu.make_async_copy(src, dst, out_sem.at[len(finals)])
        copy.start()
        finals.append(copy)

    def left_done(p):
        for m in (12, 13, 14) if p in DIRECT_GATHER else (13, 15):
            live[p, m].wait_recv()
        if p == PIECES - 1:
            keep(rg.at[p], rg_out)

    def gradient_piece(p):
        parts = piece_rows(rg[p])
        for a in range(4):
            turned = parts[a].astype(F32).T.astype(BF)
            nat[p * 4 + a] = turned
        keep(nat.at[pl.ds(p * 4, 4)], nat_out.at[pl.ds(p * 4, 4)])
        for h in range(2):
            lhs = jnp.concatenate(
                [
                    jnp.concatenate([parts[a], lht[a, pl.ds(p * 128, 128), :]], axis=1)
                    for a in (2 * h, 2 * h + 1)
                ],
                axis=0,
            )
            summed = jnp.dot(lhs, rhs[...], preferred_element_type=F32).astype(BF)
            for k in range(2):
                a = 2 * h + k

                def store(block, rows):
                    grads[a, pl.ds(p * 1024 + block * 256, 256), :] = rows

                spread_states(spread[...], summed[k * 128:(k + 1) * 128], store)
        rows = pl.ds(p * 1024, 1024)
        keep(grads.at[:, rows, :], grad_out.at[:, rows, :])

    def right_diffs(half):
        lhs = loh[pl.ds(pl.multiple_of(half * 256, 256), 256), :]
        fields = jnp.dot(lhs, flat[...], preferred_element_type=F32)
        return [fields[:, b * 256:(b + 1) * 256] - fields[:, 768:1024] for b in range(3)]

    def core_scatter():
        for b, diff in enumerate(right_diffs(1 - core)):
            cs[:, pl.ds(b * 256, 256)] = diff.astype(BF)
        live["c"] = send(cs, cr, rsems, 0, core_peer)

    def right_own():
        for b, diff in enumerate(right_diffs(core)):
            own[:, pl.ds(b * 256, 256)] = diff

    def yz_scatter():
        live["c"].wait_recv()
        for c in range(8):
            rows = pl.ds(c * 32, 32)
            yp[c] = (own[rows, :] + cr[rows, :].astype(F32)).astype(BF)
        for d in (5, 4, 3, 7, 2, 6, 1):
            chunk = lax.rem(y + d // 2, 4) * 2 + lax.rem(zl + d % 2, 2)
            live["s", d] = send(yp.at[chunk], yb.at[d - 1], rsems, d, at_yz(d))

    def right_rows(start, count):
        return pl.ds(pl.multiple_of(start, 32), count)

    def yz_gather():
        for d in range(1, 8):
            live["s", d].wait_recv()
        total = yp[y * 2 + zl].astype(F32)
        for k in range(7):
            total = total + yb[k].astype(F32)
        rows = right_rows(core * 256 + y * 64 + zl * 32, 32)
        base = rbias_ref[pl.ds(3, 1), :]
        diffs = [
            total[:, b * 256:(b + 1) * 256] + (rbias_ref[pl.ds(b, 1), :] - base) for b in range(3)
        ]
        for b, part in enumerate(softmax_residual(diffs, right_ref[rows, :])):
            rr[rows, pl.ds(b * 256, 256)] = part
        block = rr.at[rows, :]
        for d in (5, 4, 3, 7, 2, 6, 1):
            live["g", d] = send(block, block, rsems, 7 + d, at_yz(d))

    def core_gather():
        for d in range(1, 8):
            live["g", d].wait_recv()
        block = rr.at[right_rows(core * 256, 256), :]
        live["c1"] = send(block, block, rsems, 15, core_peer)

    def right_done():
        live["c1"].wait_recv()
        parts = four_states([rr[:, pl.ds(b * 256, 256)] for b in range(3)])
        for b in range(4):
            rhs[pl.ds(512, 512), pl.ds(b * 256, 256)] = -parts[b]
        keep(rhs, rhs_out)

    def right_spread():
        def store(block, rows):
            rres[pl.ds(block * 256, 256), :] = rows

        spread_states(spread[...], -rhs[pl.ds(512, 512), :], store)
        keep(rres, rres_out)

    def right_onehots():
        states = right_ref[...]
        for b in range(4):
            rhs[pl.ds(0, 512), pl.ds(b * 256, 256)] = -onehot(states, b)

    def left_tables():
        left_t = left_ref[...].T
        for xc in range(4):
            slt[xc] = left_t[:, xc * 128:(xc + 1) * 128]
        for a in range(4):
            lht[a] = onehot(left_t, a)
        keep(lht.at[:, pl.ds((PIECES - 1) * 128, 128), :], lht_out)
        base = lbias_ref[pl.ds(3, 1), :]
        for a in range(3):
            diff = lbias_ref[pl.ds(a, 1), :] - base
            for p in range(PIECES):
                part = jnp.broadcast_to(diff[:, p * 128:(p + 1) * 128], (128, 128))
                bt[a, pl.ds(p * 128, 128), :] = part.T

    def left_onehots():
        states = left_ref[...]
        for a in range(4):
            loh[:, pl.ds(a * 512, 512)] = onehot(states, a)

    left_fields(0)
    pl.semaphore_wait(barrier, len(peers))
    x_scatter(0)
    for p in (1, 2, 3):
        left_fields(p)
        x_scatter(p)
    for key in ("left", "lbias", "rbias"):
        loads[key].wait()
    left_onehots()
    core_scatter()
    z_scatter(0)
    right_own()
    x_relay(1)
    yz_scatter()
    x_relay(2)
    left_tables()
    right_onehots()
    z_gather(0)
    z_scatter(1)
    x_relay(3)
    z_scatter(2)
    x_gather(0)
    z_gather(1)
    z_scatter(3)
    yz_gather()
    z_gather(2)
    x_gather(1)
    z_gather(3)
    x_forward(0)
    x_gather(2)
    core_gather()
    x_gather(3)
    x_forward(1)
    right_done()
    left_done(0)
    x_forward(2)
    gradient_piece(0)
    right_spread()
    left_done(1)
    gradient_piece(1)
    left_done(2)
    gradient_piece(2)
    left_done(3)
    for copy in sent:
        copy.wait_send()
    for copy in finals:
        copy.wait()


def exchange(left_states, right_states, left_bias, right_bias, couplings):
    hbm = pl.BlockSpec(memory_space=pltpu.HBM)
    any_space = pl.BlockSpec(memory_space=pl.ANY)
    n = PIECES
    return pl.pallas_call(
        exchange_kernel,
        out_shape=(
            jax.ShapeDtypeStruct((4, 3072, 128), BF),
            jax.ShapeDtypeStruct((12, 512, 128), BF),
            jax.ShapeDtypeStruct((4096, 128), BF),
            jax.ShapeDtypeStruct((1024, 1024), BF),
            jax.ShapeDtypeStruct((4, 4, 3, 32, 128), BF),
            jax.ShapeDtypeStruct((4, 128, 512), BF),
        ),
        in_specs=[hbm] * 5,
        out_specs=(any_space,) * 6,
        scratch_shapes=[
            pltpu.VMEM((512, 512), jnp.int32),
            pltpu.VMEM((512, 256), jnp.int32),
            pltpu.VMEM((4, 512), F32),
            pltpu.VMEM((4, 256), F32),
            pltpu.VMEM((4, 4096, 128), BF),
            pltpu.VMEM((2048, 1024), BF),
            pltpu.VMEM((256, 256), BF),
            pltpu.VMEM((256, 256), BF),
            pltpu.VMEM((4, 3072, 128), BF),
            pltpu.VMEM((12, 512, 128), BF),
            pltpu.VMEM((4096, 128), BF),
            pltpu.VMEM((1024, 1024), BF),
            pltpu.VMEM((4, 512, 512), BF),
            pltpu.VMEM((1024, 512), BF),
            pltpu.VMEM((512, 2048), BF),
            pltpu.VMEM((4, 512, 128), jnp.int32),
            pltpu.VMEM((3, 512, 128), F32),
            pltpu.VMEM((n, 4, 4, 3, 32, 128), BF),
            pltpu.VMEM((n, 2, 2, 3, 32, 128), BF),
            pltpu.VMEM((n, 3, 4, 3, 32, 128), BF),
            pltpu.VMEM((n, 4, 3, 32, 128), BF),
            pltpu.VMEM((n, 3, 3, 32, 128), BF),
            pltpu.VMEM((n, 4, 4, 3, 32, 128), BF),
            pltpu.VMEM((256, 768), BF),
            pltpu.VMEM((256, 768), BF),
            pltpu.VMEM((256, 768), F32),
            pltpu.VMEM((8, 32, 768), BF),
            pltpu.VMEM((7, 32, 768), BF),
            pltpu.VMEM((512, 768), BF),
            pltpu.SemaphoreType.DMA((n + 4,)),
            pltpu.SemaphoreType.DMA((10,)),
            pltpu.SemaphoreType.DMA((n * 16,)),
            pltpu.SemaphoreType.DMA((n * 16,)),
            pltpu.SemaphoreType.DMA((16,)),
            pltpu.SemaphoreType.DMA((16,)),
        ],
        compiler_params=pltpu.CompilerParams(
            collective_id=0, has_side_effects=True, vmem_limit_bytes=EXCHANGE_VMEM
        ),
        name="exchange",
    )(*[pltpu.with_memory_space_constraint(v, pltpu.HBM) for v in (left_states, right_states, left_bias, right_bias, couplings)])


def finish_kernel(
    part_ref, nat_ref, rres_ref, rhs_ref, rg_ref, lht_ref,
    lres_out, rres_out, grad_out,
    grads, lres, sems,
):
    copies = []

    def put(src, dst):
        copy = pltpu.make_async_copy(src, dst, sems.at[len(copies)])
        copy.start()
        copies.append(copy)

    put(part_ref, grad_out.at[:, pl.ds(0, 3072), :])
    put(rres_ref, rres_out)
    spread = permutation(5)
    gather = permutation(4)
    parts = piece_rows(rg_ref[...])

    def last_piece(h):
        lhs = jnp.concatenate(
            [jnp.concatenate([parts[a], lht_ref[a]], axis=1) for a in (2 * h, 2 * h + 1)], axis=0
        )
        summed = jnp.dot(lhs, rhs_ref[...], preferred_element_type=F32).astype(BF)
        for k in range(2):
            a = 2 * h + k

            def store(block, rows):
                grads[a, pl.ds(block * 256, 256), :] = rows

            spread_states(spread, summed[k * 128:(k + 1) * 128], store)
        states = pl.ds(2 * h, 2)
        put(grads.at[states], grad_out.at[states, pl.ds(3072, 1024), :])

    last_piece(0)
    turned = [part.astype(F32).T.astype(BF) for part in parts]
    for q in range(4):
        for h in range(4 * q, 4 * q + 4):
            stack = side_by_side(
                [
                    [nat_ref[m, pl.ds((2 * h + k) * 16, 16), :] for m in range(12)]
                    + [block[(2 * h + k) * 16:(2 * h + k + 1) * 16] for block in turned]
                    for k in range(2)
                ]
            )
            rows = jnp.dot(gather, stack, preferred_element_type=F32).astype(BF)
            for k in range(2):
                lres[pl.ds((2 * h + k) * 256, 256), :] = rows[:, k * 128:(k + 1) * 128]
        block = pl.ds(q * 2048, 2048)
        put(lres.at[block, :], lres_out.at[block, :])
    last_piece(1)
    for copy in copies:
        copy.wait()


def finish(part, nat, rres, rhs, rg, lht):
    vmem = pl.BlockSpec(memory_space=pltpu.VMEM)
    any_space = pl.BlockSpec(memory_space=pl.ANY)
    return pl.pallas_call(
        finish_kernel,
        out_shape=(
            jax.ShapeDtypeStruct((8192, 128), BF),
            jax.ShapeDtypeStruct((4096, 128), BF),
            jax.ShapeDtypeStruct((4, 4096, 128), BF),
        ),
        in_specs=[any_space, vmem, any_space, vmem, vmem, vmem],
        out_specs=(pl.BlockSpec(memory_space=pltpu.HBM),) * 3,
        scratch_shapes=[
            pltpu.VMEM((4, 1024, 128), BF),
            pltpu.VMEM((8192, 128), BF),
            pltpu.SemaphoreType.DMA((8,)),
        ],
        compiler_params=pltpu.CompilerParams(vmem_limit_bytes=FINISH_VMEM),
        name="finish",
    )(part, nat, rres, rhs, rg, lht)


def body(left_states, right_states, left_bias, right_bias, couplings):
    view = couplings.reshape(4, 512, 4, 2, 128).transpose(0, 1, 3, 2, 4).reshape(4, 4096, 128)
    kept = exchange(left_states, right_states, left_bias, right_bias, view)
    left, right, grad = finish(*kept)
    left_residual = left.reshape(512, 4, 4, 128).transpose(0, 2, 1, 3).reshape(512, 4, 512)
    right_residual = right.reshape(512, 2, 4, 128).transpose(0, 2, 1, 3).reshape(512, 4, 256)
    coupling_grad = grad.reshape(4, 512, 2, 4, 128).transpose(0, 1, 3, 2, 4).reshape(4, 512, 4, 256)
    return left_residual, right_residual, coupling_grad


def solution(mesh):
    in_specs = (
        P(None, "row"),
        P(None, "col"),
        P(None, "row"),
        P(None, "col"),
        P(None, "row", None, "col"),
    )
    out_specs = (P(None, None, "row"), P(None, None, "col"), P(None, "row", None, "col"))
    return jax.shard_map(body, mesh=mesh, in_specs=in_specs, out_specs=out_specs, check_vma=False)
```

```python
import jax
import jax.numpy as jnp
from jax import lax
from jax.experimental import pallas as pl
from jax.experimental.pallas import tpu as pltpu
from jax.sharding import PartitionSpec as P

MESH = pl.DeviceIdType.MESH
BF = jnp.bfloat16
F32 = jnp.float32
PIECES = 4
DIRECT_SCATTER = (0,)
DIRECT_GATHER = (3,)
Z_FIRST = (1,)
EXCHANGE_VMEM = 40 * 1024 * 1024
FINISH_VMEM = 24 * 1024 * 1024


def permutation(inner_bits):
    outer_bits = 8 - inner_bits
    at = lax.broadcasted_iota(jnp.int32, (256, 256), 0)
    of = lax.broadcasted_iota(jnp.int32, (256, 256), 1)
    want = ((at & ((1 << outer_bits) - 1)) << inner_bits) + (at >> outer_bits)
    return jnp.where(of == want, 1.0, 0.0).astype(BF)


def side_by_side(blocks):
    return jnp.concatenate([jnp.concatenate(rows, axis=0) for rows in blocks], axis=1)


def spread_states(perm, values, store):
    for h in range(values.shape[0] // 64):
        stack = side_by_side(
            [
                [
                    values[(2 * h + k) * 32:(2 * h + k + 1) * 32, b * 256 + jt * 128:b * 256 + (jt + 1) * 128]
                    for jt in range(2) for b in range(4)
                ]
                for k in range(2)
            ]
        )
        turned = jnp.dot(perm, stack, preferred_element_type=F32).astype(BF)
        for k in range(2):
            store(2 * h + k, turned[:, k * 128:(k + 1) * 128])


def four_states(parts):
    last = -(parts[0].astype(F32) + parts[1].astype(F32) + parts[2].astype(F32))
    return list(parts) + [last.astype(BF)]


def piece_rows(rg):
    return four_states(
        [
            jnp.concatenate([rg[xc, :, a].reshape(128, 128) for xc in range(4)], axis=1)
            for a in range(3)
        ]
    )


def onehot(states, value):
    return jnp.where(states == value, 1.0, 0.0).astype(BF)


def softmax_residual(diffs, states):
    top = jnp.maximum(jnp.maximum(diffs[0], diffs[1]), jnp.maximum(diffs[2], 0.0))
    exps = [jnp.exp(d - top) for d in diffs]
    inverse = 1.0 / (exps[0] + exps[1] + exps[2] + jnp.exp(-top))
    return [
        (jnp.where(states == a, 1.0, 0.0) - exps[a] * inverse).astype(BF) for a in range(3)
    ]


def exchange_kernel(
    left_in, right_in, lbias_in, rbias_in, coup_ref,
    grad_out, nat_out, rres_out, rhs_out, rg_out, lht_out,
    left_ref, right_ref, lbias_ref, rbias_ref, raw, flat, perm, spread, grads, nat, rres, rhs, lht, rt, loh, slt, bt,
    lp, xa, xb, zp, zb, rg,
    cs, cr, own, yp, yb, tz, zs, zr, rr,
    in_sem, out_sem, lsend, lrecv, rsend, rrecv,
):
    row = lax.axis_index("row")
    col = lax.axis_index("col")
    core = lax.rem(row, 2)
    zl = lax.rem(lax.div(row, 2), 2)
    y = lax.div(row, 4)
    x = lax.div(col, 4)
    z = lax.rem(col, 4)

    def at_x(d):
        return {"row": row, "col": lax.rem(x + d, 4) * 4 + z}

    def at_z(d):
        return {"row": row, "col": x * 4 + lax.rem(z + d, 4)}

    def at_y(d):
        return {"row": lax.rem(y + d, 4) * 4 + zl * 2 + core, "col": col}

    core_peer = {"row": y * 4 + zl * 2 + 1 - core, "col": col}
    zl_peer = {"row": y * 4 + (1 - zl) * 2 + core, "col": col}
    peers = [at(d) for at in (at_x, at_z, at_y) for d in (1, 2, 3)] + [zl_peer, core_peer]

    def axes(p):
        return ((z, at_z), (x, at_x)) if p in Z_FIRST else ((x, at_x), (z, at_z))

    def chunk(ref, p, index, part=pl.ds(0, 4)):
        return ref.at[p, part, index] if p in Z_FIRST else ref.at[p, index, part]

    low, high = pl.ds(0, 2), pl.ds(2, 2)

    barrier = pltpu.get_barrier_semaphore()
    for peer in peers:
        pl.semaphore_signal(barrier, inc=1, device_id=peer, device_id_type=MESH)

    loads = {}

    def load(key, src, dst):
        copy = pltpu.make_async_copy(src, dst, in_sem.at[len(loads)])
        copy.start()
        loads[key] = copy

    load("right", right_in, right_ref)
    for p in range(PIECES):
        rows = pl.ds(p * 1024, 1024)
        load(p, coup_ref.at[:, rows, :], raw.at[:, rows, :])
        if p == 0:
            load("left", left_in, left_ref)
            load("lbias", lbias_in, lbias_ref)
            load("rbias", rbias_in, rbias_ref)

    sent = []

    def send(src, dst, sems, slot, peer):
        copy = pltpu.make_async_remote_copy(
            src_ref=src, dst_ref=dst, send_sem=sems[0].at[slot], recv_sem=sems[1].at[slot],
            device_id=peer, device_id_type=MESH,
        )
        copy.start()
        sent.append(copy)
        return copy

    lsems = (lsend, lrecv)
    rsems = (rsend, rrecv)

    perm[...] = permutation(3)
    spread[...] = permutation(5)
    loads["right"].wait()
    right_t = right_ref[...].T
    for b in range(4):
        rt[pl.ds(b * 256, 256), :] = onehot(right_t, b)

    live = {}

    def left_fields(p):
        loads[p].wait()
        for a in range(4):
            for h in range(2):
                pair = [
                    raw[a, pl.ds(p * 1024 + (2 * h + k) * 256, 256), :] for k in range(2)
                ]
                turned = jnp.dot(
                    perm[...], jnp.concatenate(pair, axis=1), preferred_element_type=F32
                ).astype(BF)
                for k in range(2):
                    for jt in range(2):
                        for b in range(4):
                            flat[
                                pl.ds(a * 512 + p * 128 + (2 * h + k) * 32, 32),
                                pl.ds(b * 256 + jt * 128, 128),
                            ] = turned[(jt * 4 + b) * 32:(jt * 4 + b + 1) * 32, k * 128:(k + 1) * 128]
        lhs = jnp.concatenate([flat[pl.ds(a * 512 + p * 128, 128), :] for a in range(4)], axis=0)
        fields = jnp.dot(lhs, rt[...], preferred_element_type=F32)
        for a in range(3):
            diff = (fields[a * 128:(a + 1) * 128] - fields[384:512]).astype(BF)
            for xc in range(4):
                for zc in range(4):
                    lp[p, xc, zc, a] = diff[zc * 32:(zc + 1) * 32, xc * 128:(xc + 1) * 128]

    def first_scatter(p):
        me, at = axes(p)[0]
        if p in DIRECT_SCATTER:
            for d in (2, 1, 3):
                live[p, d] = send(chunk(lp, p, lax.rem(me + d, 4)), xb.at[p, d - 1], lsems, p * 16 + d, at(d))
            return
        opp, nxt, prv = lax.rem(me + 2, 4), lax.rem(me + 1, 4), lax.rem(me + 3, 4)
        live[p, 0] = send(chunk(lp, p, opp, low), xa.at[p, 0], lsems, p * 16 + 0, at(1))
        live[p, 1] = send(chunk(lp, p, opp, high), xa.at[p, 1], lsems, p * 16 + 1, at(3))
        live[p, 2] = send(chunk(lp, p, nxt, high), xb.at[p, 0, high], lsems, p * 16 + 2, at(1))
        live[p, 3] = send(chunk(lp, p, prv, low), xb.at[p, 1, low], lsems, p * 16 + 3, at(3))

    def relay(p):
        me, at = axes(p)[0]
        mine = chunk(lp, p, lax.rem(me + 1, 4), low)
        live[p, 0].wait_recv()
        mine[...] = (mine[...].astype(F32) + xa[p, 0].astype(F32)).astype(BF)
        live[p, 4] = send(mine, xb.at[p, 0, low], lsems, p * 16 + 4, at(1))
        mine = chunk(lp, p, lax.rem(me + 3, 4), high)
        live[p, 1].wait_recv()
        mine[...] = (mine[...].astype(F32) + xa[p, 1].astype(F32)).astype(BF)
        live[p, 5] = send(mine, xb.at[p, 1, high], lsems, p * 16 + 5, at(3))

    def second_scatter(p):
        (first, _), (me, at) = axes(p)
        direct = p in DIRECT_SCATTER
        for m in (1, 2, 3) if direct else (2, 3, 4, 5):
            live[p, m].wait_recv()
        total = chunk(lp, p, first)[...].astype(F32) + xb[p, 0].astype(F32) + xb[p, 1].astype(F32)
        if direct:
            total = total + xb[p, 2].astype(F32)
        zp[p] = total.astype(BF)
        for d in (2, 1, 3):
            live[p, 5 + d] = send(zp.at[p, lax.rem(me + d, 4)], zb.at[p, d - 1], lsems, p * 16 + 5 + d, at(d))

    def first_gather(p):
        me, at = axes(p)[1]
        for m in (6, 7, 8):
            live[p, m].wait_recv()
        total = zp[p, me].astype(F32)
        for k in range(3):
            total = total + zb[p, k].astype(F32)
        rows = pl.ds(pl.multiple_of(p * 128 + z * 32, 32), 32)
        diffs = [total[a] + bt[a, rows, :] for a in range(3)]
        result = softmax_residual(diffs, slt[x, rows, :])
        for a in range(3):
            rg[p, x, z, a] = result[a]
        block = rg.at[p, x, z]
        for d in (2, 1, 3):
            live[p, 8 + d] = send(block, block, lsems, p * 16 + 8 + d, at(d))

    def second_gather(p):
        me, at = axes(p)[0]
        for m in (9, 10, 11):
            live[p, m].wait_recv()
        block = chunk(rg, p, me)
        for d in (2, 1, 3) if p in DIRECT_GATHER else (1, 3):
            live[p, 11 + d] = send(block, block, lsems, p * 16 + 11 + d, at(d))

    def forward(p):
        me, at = axes(p)[0]
        live[p, 12].wait_recv()
        block = chunk(rg, p, lax.rem(me + 3, 4), low)
        live[p, 13] = send(block, block, lsems, p * 16 + 13, at(1))
        live[p, 14].wait_recv()
        block = chunk(rg, p, lax.rem(me + 1, 4), high)
        live[p, 15] = send(block, block, lsems, p * 16 + 15, at(3))

    finals = []

    def keep(src, dst):
        copy = pltpu.make_async_copy(src, dst, out_sem.at[len(finals)])
        copy.start()
        finals.append(copy)

    def left_done(p):
        for m in (12, 13, 14) if p in DIRECT_GATHER else (13, 15):
            live[p, m].wait_recv()
        if p == PIECES - 1:
            keep(rg.at[p], rg_out)

    def gradient_piece(p):
        parts = piece_rows(rg[p])
        for a in range(4):
            turned = parts[a].astype(F32).T.astype(BF)
            nat[p * 4 + a] = turned
        keep(nat.at[pl.ds(p * 4, 4)], nat_out.at[pl.ds(p * 4, 4)])
        for h in range(2):
            lhs = jnp.concatenate(
                [
                    jnp.concatenate([parts[a], lht[a, pl.ds(p * 128, 128), :]], axis=1)
                    for a in (2 * h, 2 * h + 1)
                ],
                axis=0,
            )
            summed = jnp.dot(lhs, rhs[...], preferred_element_type=F32).astype(BF)
            for k in range(2):
                a = 2 * h + k

                def store(block, rows):
                    grads[a, pl.ds(p * 1024 + block * 256, 256), :] = rows

                spread_states(spread[...], summed[k * 128:(k + 1) * 128], store)
        rows = pl.ds(p * 1024, 1024)
        keep(grads.at[:, rows, :], grad_out.at[:, rows, :])

    def right_diffs(half):
        lhs = loh[pl.ds(pl.multiple_of(half * 256, 256), 256), :]
        fields = jnp.dot(lhs, flat[...], preferred_element_type=F32)
        return [fields[:, b * 256:(b + 1) * 256] - fields[:, 768:1024] for b in range(3)]

    def core_scatter():
        for b, diff in enumerate(right_diffs(1 - core)):
            cs[:, pl.ds(b * 256, 256)] = diff.astype(BF)
        live["c"] = send(cs, cr, rsems, 0, core_peer)

    def right_own():
        for b, diff in enumerate(right_diffs(core)):
            own[:, pl.ds(b * 256, 256)] = diff

    def y_scatter():
        live["c"].wait_recv()
        for c in range(4):
            rows = pl.ds(c * 64, 64)
            yp[c] = (own[rows, :] + cr[rows, :].astype(F32)).astype(BF)
        for d in (2, 1, 3):
            live["ys", d] = send(yp.at[lax.rem(y + d, 4)], yb.at[d - 1], rsems, d, at_y(d))

    def zl_scatter():
        for d in (1, 2, 3):
            live["ys", d].wait_recv()
        total = yp[y].astype(F32)
        for k in range(3):
            total = total + yb[k].astype(F32)
        tz[0] = total[:32]
        tz[1] = total[32:]
        zs[...] = tz[1 - zl].astype(BF)
        live["zs"] = send(zs, zr, rsems, 4, zl_peer)

    def right_rows(start, count):
        return pl.ds(pl.multiple_of(start, 32), count)

    def zl_gather():
        live["zs"].wait_recv()
        total = tz[zl] + zr[...].astype(F32)
        rows = right_rows(core * 256 + y * 64 + zl * 32, 32)
        base = rbias_ref[pl.ds(3, 1), :]
        diffs = [
            total[:, b * 256:(b + 1) * 256] + (rbias_ref[pl.ds(b, 1), :] - base) for b in range(3)
        ]
        for b, part in enumerate(softmax_residual(diffs, right_ref[rows, :])):
            rr[rows, pl.ds(b * 256, 256)] = part
        block = rr.at[rows, :]
        live["zg"] = send(block, block, rsems, 5, zl_peer)

    def y_gather():
        live["zg"].wait_recv()
        block = rr.at[right_rows(core * 256 + y * 64, 64), :]
        for d in (2, 1, 3):
            live["yg", d] = send(block, block, rsems, 5 + d, at_y(d))

    def core_gather():
        for d in (1, 2, 3):
            live["yg", d].wait_recv()
        block = rr.at[right_rows(core * 256, 256), :]
        live["c1"] = send(block, block, rsems, 9, core_peer)

    def right_done():
        live["c1"].wait_recv()
        parts = four_states([rr[:, pl.ds(b * 256, 256)] for b in range(3)])
        for b in range(4):
            rhs[pl.ds(512, 512), pl.ds(b * 256, 256)] = -parts[b]
        keep(rhs, rhs_out)

    def right_spread():
        def store(block, rows):
            rres[pl.ds(block * 256, 256), :] = rows

        spread_states(spread[...], -rhs[pl.ds(512, 512), :], store)
        keep(rres, rres_out)

    def right_onehots():
        states = right_ref[...]
        for b in range(4):
            rhs[pl.ds(0, 512), pl.ds(b * 256, 256)] = -onehot(states, b)

    def left_tables():
        left_t = left_ref[...].T
        for xc in range(4):
            slt[xc] = left_t[:, xc * 128:(xc + 1) * 128]
        for a in range(4):
            lht[a] = onehot(left_t, a)
        keep(lht.at[:, pl.ds((PIECES - 1) * 128, 128), :], lht_out)
        base = lbias_ref[pl.ds(3, 1), :]
        for a in range(3):
            diff = lbias_ref[pl.ds(a, 1), :] - base
            for p in range(PIECES):
                part = jnp.broadcast_to(diff[:, p * 128:(p + 1) * 128], (128, 128))
                bt[a, pl.ds(p * 128, 128), :] = part.T

    def left_onehots():
        states = left_ref[...]
        for a in range(4):
            loh[:, pl.ds(a * 512, 512)] = onehot(states, a)

    left_fields(0)
    for key in ("left", "lbias", "rbias"):
        loads[key].wait()
    left_onehots()
    pl.semaphore_wait(barrier, len(peers))
    first_scatter(0)
    left_fields(1)
    left_fields(2)
    first_scatter(1)
    first_scatter(2)
    left_fields(3)
    core_scatter()
    right_own()
    left_tables()
    second_scatter(0)
    relay(2)
    relay(1)
    y_scatter()
    first_scatter(3)
    second_scatter(2)
    first_gather(0)
    second_scatter(1)
    relay(3)
    zl_scatter()
    first_gather(2)
    first_gather(1)
    second_gather(0)
    zl_gather()
    right_onehots()
    second_scatter(3)
    second_gather(1)
    y_gather()
    second_gather(2)
    forward(0)
    first_gather(3)
    forward(2)
    forward(1)
    core_gather()
    second_gather(3)
    left_done(0)
    left_done(2)
    right_done()
    gradient_piece(0)
    right_spread()
    left_done(1)
    gradient_piece(2)
    gradient_piece(1)
    left_done(3)
    for copy in sent:
        copy.wait_send()
    for copy in finals:
        copy.wait()


def exchange(left_states, right_states, left_bias, right_bias, couplings):
    hbm = pl.BlockSpec(memory_space=pltpu.HBM)
    any_space = pl.BlockSpec(memory_space=pl.ANY)
    n = PIECES
    return pl.pallas_call(
        exchange_kernel,
        out_shape=(
            jax.ShapeDtypeStruct((4, 3072, 128), BF),
            jax.ShapeDtypeStruct((12, 512, 128), BF),
            jax.ShapeDtypeStruct((4096, 128), BF),
            jax.ShapeDtypeStruct((1024, 1024), BF),
            jax.ShapeDtypeStruct((4, 4, 3, 32, 128), BF),
            jax.ShapeDtypeStruct((4, 128, 512), BF),
        ),
        in_specs=[hbm] * 5,
        out_specs=(any_space,) * 6,
        scratch_shapes=[
            pltpu.VMEM((512, 512), jnp.int32),
            pltpu.VMEM((512, 256), jnp.int32),
            pltpu.VMEM((4, 512), F32),
            pltpu.VMEM((4, 256), F32),
            pltpu.VMEM((4, 4096, 128), BF),
            pltpu.VMEM((2048, 1024), BF),
            pltpu.VMEM((256, 256), BF),
            pltpu.VMEM((256, 256), BF),
            pltpu.VMEM((4, 3072, 128), BF),
            pltpu.VMEM((12, 512, 128), BF),
            pltpu.VMEM((4096, 128), BF),
            pltpu.VMEM((1024, 1024), BF),
            pltpu.VMEM((4, 512, 512), BF),
            pltpu.VMEM((1024, 512), BF),
            pltpu.VMEM((512, 2048), BF),
            pltpu.VMEM((4, 512, 128), jnp.int32),
            pltpu.VMEM((3, 512, 128), F32),
            pltpu.VMEM((n, 4, 4, 3, 32, 128), BF),
            pltpu.VMEM((n, 2, 2, 3, 32, 128), BF),
            pltpu.VMEM((n, 3, 4, 3, 32, 128), BF),
            pltpu.VMEM((n, 4, 3, 32, 128), BF),
            pltpu.VMEM((n, 3, 3, 32, 128), BF),
            pltpu.VMEM((n, 4, 4, 3, 32, 128), BF),
            pltpu.VMEM((256, 768), BF),
            pltpu.VMEM((256, 768), BF),
            pltpu.VMEM((256, 768), F32),
            pltpu.VMEM((4, 64, 768), BF),
            pltpu.VMEM((3, 64, 768), BF),
            pltpu.VMEM((2, 32, 768), F32),
            pltpu.VMEM((32, 768), BF),
            pltpu.VMEM((32, 768), BF),
            pltpu.VMEM((512, 768), BF),
            pltpu.SemaphoreType.DMA((n + 4,)),
            pltpu.SemaphoreType.DMA((10,)),
            pltpu.SemaphoreType.DMA((n * 16,)),
            pltpu.SemaphoreType.DMA((n * 16,)),
            pltpu.SemaphoreType.DMA((10,)),
            pltpu.SemaphoreType.DMA((10,)),
        ],
        compiler_params=pltpu.CompilerParams(
            collective_id=0, has_side_effects=True, vmem_limit_bytes=EXCHANGE_VMEM
        ),
        name="exchange",
    )(*[pltpu.with_memory_space_constraint(v, pltpu.HBM) for v in (left_states, right_states, left_bias, right_bias, couplings)])


def finish_kernel(
    part_ref, nat_ref, rres_ref, rhs_ref, rg_ref, lht_ref,
    lres_out, rres_out, grad_out,
    grads, lres, sems,
):
    copies = []

    def put(src, dst):
        copy = pltpu.make_async_copy(src, dst, sems.at[len(copies)])
        copy.start()
        copies.append(copy)

    put(part_ref, grad_out.at[:, pl.ds(0, 3072), :])
    put(rres_ref, rres_out)
    spread = permutation(5)
    gather = permutation(4)
    parts = piece_rows(rg_ref[...])

    def last_piece(h):
        lhs = jnp.concatenate(
            [jnp.concatenate([parts[a], lht_ref[a]], axis=1) for a in (2 * h, 2 * h + 1)], axis=0
        )
        summed = jnp.dot(lhs, rhs_ref[...], preferred_element_type=F32).astype(BF)
        for k in range(2):
            a = 2 * h + k

            def store(block, rows):
                grads[a, pl.ds(block * 256, 256), :] = rows

            spread_states(spread, summed[k * 128:(k + 1) * 128], store)
        states = pl.ds(2 * h, 2)
        put(grads.at[states], grad_out.at[states, pl.ds(3072, 1024), :])

    last_piece(0)
    turned = [part.astype(F32).T.astype(BF) for part in parts]
    for q in range(4):
        for h in range(4 * q, 4 * q + 4):
            stack = side_by_side(
                [
                    [nat_ref[m, pl.ds((2 * h + k) * 16, 16), :] for m in range(12)]
                    + [block[(2 * h + k) * 16:(2 * h + k + 1) * 16] for block in turned]
                    for k in range(2)
                ]
            )
            rows = jnp.dot(gather, stack, preferred_element_type=F32).astype(BF)
            for k in range(2):
                lres[pl.ds((2 * h + k) * 256, 256), :] = rows[:, k * 128:(k + 1) * 128]
        block = pl.ds(q * 2048, 2048)
        put(lres.at[block, :], lres_out.at[block, :])
    last_piece(1)
    for copy in copies:
        copy.wait()


def finish(part, nat, rres, rhs, rg, lht):
    vmem = pl.BlockSpec(memory_space=pltpu.VMEM)
    any_space = pl.BlockSpec(memory_space=pl.ANY)
    return pl.pallas_call(
        finish_kernel,
        out_shape=(
            jax.ShapeDtypeStruct((8192, 128), BF),
            jax.ShapeDtypeStruct((4096, 128), BF),
            jax.ShapeDtypeStruct((4, 4096, 128), BF),
        ),
        in_specs=[any_space, vmem, any_space, vmem, vmem, vmem],
        out_specs=(pl.BlockSpec(memory_space=pltpu.HBM),) * 3,
        scratch_shapes=[
            pltpu.VMEM((4, 1024, 128), BF),
            pltpu.VMEM((8192, 128), BF),
            pltpu.SemaphoreType.DMA((8,)),
        ],
        compiler_params=pltpu.CompilerParams(vmem_limit_bytes=FINISH_VMEM),
        name="finish",
    )(part, nat, rres, rhs, rg, lht)


def body(left_states, right_states, left_bias, right_bias, couplings):
    view = couplings.reshape(4, 512, 4, 2, 128).transpose(0, 1, 3, 2, 4).reshape(4, 4096, 128)
    kept = exchange(left_states, right_states, left_bias, right_bias, view)
    left, right, grad = finish(*kept)
    left_residual = left.reshape(512, 4, 4, 128).transpose(0, 2, 1, 3).reshape(512, 4, 512)
    right_residual = right.reshape(512, 2, 4, 128).transpose(0, 2, 1, 3).reshape(512, 4, 256)
    coupling_grad = grad.reshape(4, 512, 2, 4, 128).transpose(0, 1, 3, 2, 4).reshape(4, 512, 4, 256)
    return left_residual, right_residual, coupling_grad


def solution(mesh):
    in_specs = (
        P(None, "row"),
        P(None, "col"),
        P(None, "row"),
        P(None, "col"),
        P(None, "row", None, "col"),
    )
    out_specs = (P(None, None, "row"), P(None, None, "col"), P(None, "row", None, "col"))
    return jax.shard_map(body, mesh=mesh, in_specs=in_specs, out_specs=out_specs, check_vma=False)
```

```python
import jax
import jax.numpy as jnp
from jax import lax
from jax.experimental import pallas as pl
from jax.experimental.pallas import tpu as pltpu
from jax.sharding import PartitionSpec as P

MESH = pl.DeviceIdType.MESH
BF = jnp.bfloat16
F32 = jnp.float32
PIECES = 4
DIRECT_SCATTER = (0,)
DIRECT_GATHER = (0, 3)
Z_FIRST = (1,)
EXCHANGE_VMEM = 40 * 1024 * 1024
FINISH_VMEM = 24 * 1024 * 1024


def permutation(inner_bits):
    outer_bits = 8 - inner_bits
    at = lax.broadcasted_iota(jnp.int32, (256, 256), 0)
    of = lax.broadcasted_iota(jnp.int32, (256, 256), 1)
    want = ((at & ((1 << outer_bits) - 1)) << inner_bits) + (at >> outer_bits)
    return jnp.where(of == want, 1.0, 0.0).astype(BF)


def side_by_side(blocks):
    return jnp.concatenate([jnp.concatenate(rows, axis=0) for rows in blocks], axis=1)


def spread_states(perm, values, store):
    for h in range(values.shape[0] // 64):
        stack = side_by_side(
            [
                [
                    values[(2 * h + k) * 32:(2 * h + k + 1) * 32, b * 256 + jt * 128:b * 256 + (jt + 1) * 128]
                    for jt in range(2) for b in range(4)
                ]
                for k in range(2)
            ]
        )
        turned = jnp.dot(perm, stack, preferred_element_type=F32).astype(BF)
        for k in range(2):
            store(2 * h + k, turned[:, k * 128:(k + 1) * 128])


def four_states(parts):
    last = -(parts[0].astype(F32) + parts[1].astype(F32) + parts[2].astype(F32))
    return list(parts) + [last.astype(BF)]


def piece_rows(rg):
    return four_states(
        [
            jnp.concatenate([rg[xc, :, a].reshape(128, 128) for xc in range(4)], axis=1)
            for a in range(3)
        ]
    )


def onehot(states, value):
    return jnp.where(states == value, 1.0, 0.0).astype(BF)


def piece_gradient(parts, heads, rhs, right_sum):
    lhs = jnp.concatenate(
        [jnp.concatenate([parts[a], heads[a]], axis=1) for a in range(3)], axis=0
    )
    nine = jnp.dot(lhs, rhs[:, pl.ds(0, 768)], preferred_element_type=F32)
    sums = [jnp.sum(parts[a].astype(F32), axis=1, keepdims=True) for a in range(3)]
    blocks = []
    for a in range(3):
        row = [nine[a * 128:(a + 1) * 128, b * 256:(b + 1) * 256] for b in range(3)]
        blocks.append(row + [-sums[a] - (row[0] + row[1] + row[2])])
    last = [
        right_sum[pl.ds(0, 1), pl.ds(b * 256, 256)] - (blocks[0][b] + blocks[1][b] + blocks[2][b])
        for b in range(3)
    ]
    blocks.append(last + [(sums[0] + sums[1] + sums[2]) - (last[0] + last[1] + last[2])])
    return [jnp.concatenate([block.astype(BF) for block in row], axis=1) for row in blocks]


def softmax_residual(diffs, states):
    top = jnp.maximum(jnp.maximum(diffs[0], diffs[1]), jnp.maximum(diffs[2], 0.0))
    exps = [jnp.exp(d - top) for d in diffs]
    inverse = 1.0 / (exps[0] + exps[1] + exps[2] + jnp.exp(-top))
    return [
        (jnp.where(states == a, 1.0, 0.0) - exps[a] * inverse).astype(BF) for a in range(3)
    ]


def exchange_kernel(
    left_in, right_in, lbias_in, rbias_in, coup_ref,
    grad_out, nat_out, rres_out, rhs_out, rg_out, lht_out,
    left_ref, right_ref, lbias_ref, rbias_ref, raw, flat, perm, spread, grads, nat, rres, rhs, rsum, lht, rt, loh, slt, bt,
    lp, xa, xb, zp, zb, rg,
    cs, cr, own, yp, yb, tz, zs, zr, rr,
    in_sem, out_sem, lsend, lrecv, rsend, rrecv,
):
    row = lax.axis_index("row")
    col = lax.axis_index("col")
    core = lax.rem(row, 2)
    zl = lax.rem(lax.div(row, 2), 2)
    y = lax.div(row, 4)
    x = lax.div(col, 4)
    z = lax.rem(col, 4)

    def at_x(d):
        return {"row": row, "col": lax.rem(x + d, 4) * 4 + z}

    def at_z(d):
        return {"row": row, "col": x * 4 + lax.rem(z + d, 4)}

    def at_y(d):
        return {"row": lax.rem(y + d, 4) * 4 + zl * 2 + core, "col": col}

    core_peer = {"row": y * 4 + zl * 2 + 1 - core, "col": col}
    zl_peer = {"row": y * 4 + (1 - zl) * 2 + core, "col": col}
    peers = [at(d) for at in (at_x, at_z, at_y) for d in (1, 2, 3)] + [zl_peer, core_peer]

    def axes(p):
        return ((z, at_z), (x, at_x)) if p in Z_FIRST else ((x, at_x), (z, at_z))

    def chunk(ref, p, index, part=pl.ds(0, 4)):
        return ref.at[p, part, index] if p in Z_FIRST else ref.at[p, index, part]

    low, high = pl.ds(0, 2), pl.ds(2, 2)

    barrier = pltpu.get_barrier_semaphore()
    for peer in peers:
        pl.semaphore_signal(barrier, inc=1, device_id=peer, device_id_type=MESH)

    loads = {}

    def load(key, src, dst):
        copy = pltpu.make_async_copy(src, dst, in_sem.at[len(loads)])
        copy.start()
        loads[key] = copy

    load("right", right_in, right_ref)
    for p in range(PIECES):
        rows = pl.ds(p * 1024, 1024)
        load(p, coup_ref.at[:, rows, :], raw.at[:, rows, :])
        if p == 0:
            load("left", left_in, left_ref)
            load("lbias", lbias_in, lbias_ref)
            load("rbias", rbias_in, rbias_ref)

    sent = []

    def send(src, dst, sems, slot, peer):
        copy = pltpu.make_async_remote_copy(
            src_ref=src, dst_ref=dst, send_sem=sems[0].at[slot], recv_sem=sems[1].at[slot],
            device_id=peer, device_id_type=MESH,
        )
        copy.start()
        sent.append(copy)
        return copy

    lsems = (lsend, lrecv)
    rsems = (rsend, rrecv)

    perm[...] = permutation(3)
    spread[...] = permutation(5)
    loads["right"].wait()
    right_t = right_ref[...].T
    for b in range(4):
        rt[pl.ds(b * 256, 256), :] = onehot(right_t, b)

    live = {}

    def left_fields(p):
        loads[p].wait()
        for a in range(4):
            for h in range(2):
                pair = [
                    raw[a, pl.ds(p * 1024 + (2 * h + k) * 256, 256), :] for k in range(2)
                ]
                turned = jnp.dot(
                    perm[...], jnp.concatenate(pair, axis=1), preferred_element_type=F32
                ).astype(BF)
                for k in range(2):
                    for jt in range(2):
                        for b in range(4):
                            flat[
                                pl.ds(a * 512 + p * 128 + (2 * h + k) * 32, 32),
                                pl.ds(b * 256 + jt * 128, 128),
                            ] = turned[(jt * 4 + b) * 32:(jt * 4 + b + 1) * 32, k * 128:(k + 1) * 128]
        lhs = jnp.concatenate([flat[pl.ds(a * 512 + p * 128, 128), :] for a in range(4)], axis=0)
        fields = jnp.dot(lhs, rt[...], preferred_element_type=F32)
        for a in range(3):
            diff = (fields[a * 128:(a + 1) * 128] - fields[384:512]).astype(BF)
            for xc in range(4):
                for zc in range(4):
                    lp[p, xc, zc, a] = diff[zc * 32:(zc + 1) * 32, xc * 128:(xc + 1) * 128]

    def first_scatter(p):
        me, at = axes(p)[0]
        if p in DIRECT_SCATTER:
            for d in (2, 1, 3):
                live[p, d] = send(chunk(lp, p, lax.rem(me + d, 4)), xb.at[p, d - 1], lsems, p * 16 + d, at(d))
            return
        opp, nxt, prv = lax.rem(me + 2, 4), lax.rem(me + 1, 4), lax.rem(me + 3, 4)
        live[p, 0] = send(chunk(lp, p, opp, low), xa.at[p, 0], lsems, p * 16 + 0, at(1))
        live[p, 1] = send(chunk(lp, p, opp, high), xa.at[p, 1], lsems, p * 16 + 1, at(3))
        live[p, 2] = send(chunk(lp, p, nxt, high), xb.at[p, 0, high], lsems, p * 16 + 2, at(1))
        live[p, 3] = send(chunk(lp, p, prv, low), xb.at[p, 1, low], lsems, p * 16 + 3, at(3))

    def relay(p):
        me, at = axes(p)[0]
        mine = chunk(lp, p, lax.rem(me + 1, 4), low)
        live[p, 0].wait_recv()
        mine[...] = (mine[...].astype(F32) + xa[p, 0].astype(F32)).astype(BF)
        live[p, 4] = send(mine, xb.at[p, 0, low], lsems, p * 16 + 4, at(1))
        mine = chunk(lp, p, lax.rem(me + 3, 4), high)
        live[p, 1].wait_recv()
        mine[...] = (mine[...].astype(F32) + xa[p, 1].astype(F32)).astype(BF)
        live[p, 5] = send(mine, xb.at[p, 1, high], lsems, p * 16 + 5, at(3))

    def second_scatter(p):
        (first, _), (me, at) = axes(p)
        direct = p in DIRECT_SCATTER
        for m in (1, 2, 3) if direct else (2, 3, 4, 5):
            live[p, m].wait_recv()
        total = chunk(lp, p, first)[...].astype(F32) + xb[p, 0].astype(F32) + xb[p, 1].astype(F32)
        if direct:
            total = total + xb[p, 2].astype(F32)
        zp[p] = total.astype(BF)
        for d in (2, 1, 3):
            live[p, 5 + d] = send(zp.at[p, lax.rem(me + d, 4)], zb.at[p, d - 1], lsems, p * 16 + 5 + d, at(d))

    def first_gather(p):
        me, at = axes(p)[1]
        for m in (6, 7, 8):
            live[p, m].wait_recv()
        total = zp[p, me].astype(F32)
        for k in range(3):
            total = total + zb[p, k].astype(F32)
        rows = pl.ds(pl.multiple_of(p * 128 + z * 32, 32), 32)
        diffs = [total[a] + bt[a, rows, :] for a in range(3)]
        result = softmax_residual(diffs, slt[x, rows, :])
        for a in range(3):
            rg[p, x, z, a] = result[a]
        block = rg.at[p, x, z]
        for d in (2, 1, 3):
            live[p, 8 + d] = send(block, block, lsems, p * 16 + 8 + d, at(d))

    def second_gather(p):
        me, at = axes(p)[0]
        for m in (9, 10, 11):
            live[p, m].wait_recv()
        block = chunk(rg, p, me)
        for d in (2, 1, 3) if p in DIRECT_GATHER else (1, 3):
            live[p, 11 + d] = send(block, block, lsems, p * 16 + 11 + d, at(d))

    def forward(p):
        me, at = axes(p)[0]
        live[p, 12].wait_recv()
        block = chunk(rg, p, lax.rem(me + 3, 4), low)
        live[p, 13] = send(block, block, lsems, p * 16 + 13, at(1))
        live[p, 14].wait_recv()
        block = chunk(rg, p, lax.rem(me + 1, 4), high)
        live[p, 15] = send(block, block, lsems, p * 16 + 15, at(3))

    finals = []

    def keep(src, dst):
        copy = pltpu.make_async_copy(src, dst, out_sem.at[len(finals)])
        copy.start()
        finals.append(copy)

    def left_done(p):
        for m in (12, 13, 14) if p in DIRECT_GATHER else (13, 15):
            live[p, m].wait_recv()
        if p == PIECES - 1:
            keep(rg.at[p], rg_out)

    def gradient_piece(p):
        parts = piece_rows(rg[p])
        for a in range(4):
            turned = parts[a].astype(F32).T.astype(BF)
            nat[p * 4 + a] = turned
        keep(nat.at[pl.ds(p * 4, 4)], nat_out.at[pl.ds(p * 4, 4)])
        heads = [lht[a, pl.ds(p * 128, 128), :] for a in range(3)]
        for a, values in enumerate(piece_gradient(parts, heads, rhs, rsum)):

            def store(block, rows):
                grads[a, pl.ds(p * 1024 + block * 256, 256), :] = rows

            spread_states(spread[...], values, store)
        rows = pl.ds(p * 1024, 1024)
        keep(grads.at[:, rows, :], grad_out.at[:, rows, :])

    def right_diffs(half):
        lhs = loh[pl.ds(pl.multiple_of(half * 256, 256), 256), :]
        fields = jnp.dot(lhs, flat[...], preferred_element_type=F32)
        return [fields[:, b * 256:(b + 1) * 256] - fields[:, 768:1024] for b in range(3)]

    def core_scatter():
        for b, diff in enumerate(right_diffs(1 - core)):
            cs[:, pl.ds(b * 256, 256)] = diff.astype(BF)
        live["c"] = send(cs, cr, rsems, 0, core_peer)

    def right_own():
        for b, diff in enumerate(right_diffs(core)):
            own[:, pl.ds(b * 256, 256)] = diff

    def y_scatter():
        live["c"].wait_recv()
        for c in range(4):
            rows = pl.ds(c * 64, 64)
            yp[c] = (own[rows, :] + cr[rows, :].astype(F32)).astype(BF)
        for d in (2, 1, 3):
            live["ys", d] = send(yp.at[lax.rem(y + d, 4)], yb.at[d - 1], rsems, d, at_y(d))

    def zl_scatter():
        for d in (1, 2, 3):
            live["ys", d].wait_recv()
        total = yp[y].astype(F32)
        for k in range(3):
            total = total + yb[k].astype(F32)
        tz[0] = total[:32]
        tz[1] = total[32:]
        zs[...] = tz[1 - zl].astype(BF)
        live["zs"] = send(zs, zr, rsems, 4, zl_peer)

    def right_rows(start, count):
        return pl.ds(pl.multiple_of(start, 32), count)

    def zl_gather():
        live["zs"].wait_recv()
        total = tz[zl] + zr[...].astype(F32)
        rows = right_rows(core * 256 + y * 64 + zl * 32, 32)
        base = rbias_ref[pl.ds(3, 1), :]
        diffs = [
            total[:, b * 256:(b + 1) * 256] + (rbias_ref[pl.ds(b, 1), :] - base) for b in range(3)
        ]
        for b, part in enumerate(softmax_residual(diffs, right_ref[rows, :])):
            rr[rows, pl.ds(b * 256, 256)] = part
        block = rr.at[rows, :]
        live["zg"] = send(block, block, rsems, 5, zl_peer)

    def y_gather():
        live["zg"].wait_recv()
        block = rr.at[right_rows(core * 256 + y * 64, 64), :]
        for d in (2, 1, 3):
            live["yg", d] = send(block, block, rsems, 5 + d, at_y(d))

    def core_gather():
        for d in (1, 2, 3):
            live["yg", d].wait_recv()
        block = rr.at[right_rows(core * 256, 256), :]
        live["c1"] = send(block, block, rsems, 9, core_peer)

    def right_done():
        live["c1"].wait_recv()
        parts = four_states([rr[:, pl.ds(b * 256, 256)] for b in range(3)])
        for b in range(4):
            rhs[pl.ds(512, 512), pl.ds(b * 256, 256)] = -parts[b]
        for b in range(3):
            total = jnp.sum(-parts[b].astype(F32), axis=0, keepdims=True)
            rsum[:, pl.ds(b * 256, 256)] = jnp.broadcast_to(total, (8, 256))
        keep(rhs, rhs_out)

    def right_spread():
        def store(block, rows):
            rres[pl.ds(block * 256, 256), :] = rows

        spread_states(spread[...], -rhs[pl.ds(512, 512), :], store)
        keep(rres, rres_out)

    def right_onehots():
        states = right_ref[...]
        for b in range(4):
            rhs[pl.ds(0, 512), pl.ds(b * 256, 256)] = -onehot(states, b)

    def left_tables():
        left_t = left_ref[...].T
        for xc in range(4):
            slt[xc] = left_t[:, xc * 128:(xc + 1) * 128]
        for a in range(4):
            lht[a] = onehot(left_t, a)
        keep(lht.at[:, pl.ds((PIECES - 1) * 128, 128), :], lht_out)
        base = lbias_ref[pl.ds(3, 1), :]
        for a in range(3):
            diff = lbias_ref[pl.ds(a, 1), :] - base
            for p in range(PIECES):
                part = jnp.broadcast_to(diff[:, p * 128:(p + 1) * 128], (128, 128))
                bt[a, pl.ds(p * 128, 128), :] = part.T

    def left_onehots():
        states = left_ref[...]
        for a in range(4):
            loh[:, pl.ds(a * 512, 512)] = onehot(states, a)

    left_fields(0)
    pl.semaphore_wait(barrier, len(peers))
    first_scatter(0)
    left_fields(1)
    first_scatter(1)
    left_fields(2)
    left_fields(3)
    first_scatter(2)
    for key in ("left", "lbias", "rbias"):
        loads[key].wait()
    left_onehots()
    core_scatter()
    first_scatter(3)
    second_scatter(0)
    right_own()
    relay(2)
    y_scatter()
    right_onehots()
    relay(1)
    second_scatter(2)
    left_tables()
    first_gather(0)
    relay(3)
    second_scatter(1)
    zl_scatter()
    first_gather(2)
    first_gather(1)
    zl_gather()
    second_gather(0)
    second_scatter(3)
    second_gather(1)
    second_gather(2)
    y_gather()
    first_gather(3)
    forward(2)
    core_gather()
    forward(1)
    second_gather(3)
    left_done(0)
    left_done(2)
    right_done()
    right_spread()
    gradient_piece(2)
    left_done(1)
    gradient_piece(1)
    gradient_piece(0)
    left_done(3)
    for copy in sent:
        copy.wait_send()
    for copy in finals:
        copy.wait()


def exchange(left_states, right_states, left_bias, right_bias, couplings):
    hbm = pl.BlockSpec(memory_space=pltpu.HBM)
    any_space = pl.BlockSpec(memory_space=pl.ANY)
    n = PIECES
    return pl.pallas_call(
        exchange_kernel,
        out_shape=(
            jax.ShapeDtypeStruct((4, 3072, 128), BF),
            jax.ShapeDtypeStruct((12, 512, 128), BF),
            jax.ShapeDtypeStruct((4096, 128), BF),
            jax.ShapeDtypeStruct((1024, 1024), BF),
            jax.ShapeDtypeStruct((4, 4, 3, 32, 128), BF),
            jax.ShapeDtypeStruct((4, 128, 512), BF),
        ),
        in_specs=[hbm] * 5,
        out_specs=(any_space,) * 6,
        scratch_shapes=[
            pltpu.VMEM((512, 512), jnp.int32),
            pltpu.VMEM((512, 256), jnp.int32),
            pltpu.VMEM((4, 512), F32),
            pltpu.VMEM((4, 256), F32),
            pltpu.VMEM((4, 4096, 128), BF),
            pltpu.VMEM((2048, 1024), BF),
            pltpu.VMEM((256, 256), BF),
            pltpu.VMEM((256, 256), BF),
            pltpu.VMEM((4, 3072, 128), BF),
            pltpu.VMEM((12, 512, 128), BF),
            pltpu.VMEM((4096, 128), BF),
            pltpu.VMEM((1024, 1024), BF),
            pltpu.VMEM((8, 768), F32),
            pltpu.VMEM((4, 512, 512), BF),
            pltpu.VMEM((1024, 512), BF),
            pltpu.VMEM((512, 2048), BF),
            pltpu.VMEM((4, 512, 128), jnp.int32),
            pltpu.VMEM((3, 512, 128), F32),
            pltpu.VMEM((n, 4, 4, 3, 32, 128), BF),
            pltpu.VMEM((n, 2, 2, 3, 32, 128), BF),
            pltpu.VMEM((n, 3, 4, 3, 32, 128), BF),
            pltpu.VMEM((n, 4, 3, 32, 128), BF),
            pltpu.VMEM((n, 3, 3, 32, 128), BF),
            pltpu.VMEM((n, 4, 4, 3, 32, 128), BF),
            pltpu.VMEM((256, 768), BF),
            pltpu.VMEM((256, 768), BF),
            pltpu.VMEM((256, 768), F32),
            pltpu.VMEM((4, 64, 768), BF),
            pltpu.VMEM((3, 64, 768), BF),
            pltpu.VMEM((2, 32, 768), F32),
            pltpu.VMEM((32, 768), BF),
            pltpu.VMEM((32, 768), BF),
            pltpu.VMEM((512, 768), BF),
            pltpu.SemaphoreType.DMA((n + 4,)),
            pltpu.SemaphoreType.DMA((10,)),
            pltpu.SemaphoreType.DMA((n * 16,)),
            pltpu.SemaphoreType.DMA((n * 16,)),
            pltpu.SemaphoreType.DMA((10,)),
            pltpu.SemaphoreType.DMA((10,)),
        ],
        compiler_params=pltpu.CompilerParams(
            collective_id=0, has_side_effects=True, vmem_limit_bytes=EXCHANGE_VMEM
        ),
        name="exchange",
    )(*[pltpu.with_memory_space_constraint(v, pltpu.HBM) for v in (left_states, right_states, left_bias, right_bias, couplings)])


def finish_kernel(
    part_ref, nat_ref, rres_ref, rhs_ref, rg_ref, lht_ref,
    lres_out, rres_out, grad_out,
    grads, lres, sems,
):
    copies = []

    def put(src, dst):
        copy = pltpu.make_async_copy(src, dst, sems.at[len(copies)])
        copy.start()
        copies.append(copy)

    put(part_ref, grad_out.at[:, pl.ds(0, 3072), :])
    put(rres_ref, rres_out)
    spread = permutation(5)
    gather = permutation(4)
    parts = piece_rows(rg_ref[...])

    def last_piece(h):
        lhs = jnp.concatenate(
            [jnp.concatenate([parts[a], lht_ref[a]], axis=1) for a in (2 * h, 2 * h + 1)], axis=0
        )
        summed = jnp.dot(lhs, rhs_ref[...], preferred_element_type=F32).astype(BF)
        for k in range(2):
            a = 2 * h + k

            def store(block, rows):
                grads[a, pl.ds(block * 256, 256), :] = rows

            spread_states(spread, summed[k * 128:(k + 1) * 128], store)
        states = pl.ds(2 * h, 2)
        put(grads.at[states], grad_out.at[states, pl.ds(3072, 1024), :])

    last_piece(0)
    turned = [part.astype(F32).T.astype(BF) for part in parts]
    for q in range(4):
        for h in range(4 * q, 4 * q + 4):
            stack = side_by_side(
                [
                    [nat_ref[m, pl.ds((2 * h + k) * 16, 16), :] for m in range(12)]
                    + [block[(2 * h + k) * 16:(2 * h + k + 1) * 16] for block in turned]
                    for k in range(2)
                ]
            )
            rows = jnp.dot(gather, stack, preferred_element_type=F32).astype(BF)
            for k in range(2):
                lres[pl.ds((2 * h + k) * 256, 256), :] = rows[:, k * 128:(k + 1) * 128]
        block = pl.ds(q * 2048, 2048)
        put(lres.at[block, :], lres_out.at[block, :])
    last_piece(1)
    for copy in copies:
        copy.wait()


def finish(part, nat, rres, rhs, rg, lht):
    vmem = pl.BlockSpec(memory_space=pltpu.VMEM)
    any_space = pl.BlockSpec(memory_space=pl.ANY)
    return pl.pallas_call(
        finish_kernel,
        out_shape=(
            jax.ShapeDtypeStruct((8192, 128), BF),
            jax.ShapeDtypeStruct((4096, 128), BF),
            jax.ShapeDtypeStruct((4, 4096, 128), BF),
        ),
        in_specs=[any_space, vmem, any_space, vmem, vmem, vmem],
        out_specs=(pl.BlockSpec(memory_space=pltpu.HBM),) * 3,
        scratch_shapes=[
            pltpu.VMEM((4, 1024, 128), BF),
            pltpu.VMEM((8192, 128), BF),
            pltpu.SemaphoreType.DMA((8,)),
        ],
        compiler_params=pltpu.CompilerParams(vmem_limit_bytes=FINISH_VMEM),
        name="finish",
    )(part, nat, rres, rhs, rg, lht)


def body(left_states, right_states, left_bias, right_bias, couplings):
    view = couplings.reshape(4, 512, 4, 2, 128).transpose(0, 1, 3, 2, 4).reshape(4, 4096, 128)
    kept = exchange(left_states, right_states, left_bias, right_bias, view)
    left, right, grad = finish(*kept)
    left_residual = left.reshape(512, 4, 4, 128).transpose(0, 2, 1, 3).reshape(512, 4, 512)
    right_residual = right.reshape(512, 2, 4, 128).transpose(0, 2, 1, 3).reshape(512, 4, 256)
    coupling_grad = grad.reshape(4, 512, 2, 4, 128).transpose(0, 1, 3, 2, 4).reshape(4, 512, 4, 256)
    return left_residual, right_residual, coupling_grad


def solution(mesh):
    in_specs = (
        P(None, "row"),
        P(None, "col"),
        P(None, "row"),
        P(None, "col"),
        P(None, "row", None, "col"),
    )
    out_specs = (P(None, None, "row"), P(None, None, "col"), P(None, "row", None, "col"))
    return jax.shard_map(body, mesh=mesh, in_specs=in_specs, out_specs=out_specs, check_vma=False)
```

```python
import jax
import jax.numpy as jnp
from jax import lax
from jax.experimental import pallas as pl
from jax.experimental.pallas import tpu as pltpu
from jax.sharding import PartitionSpec as P

MESH = pl.DeviceIdType.MESH
BF = jnp.bfloat16
F32 = jnp.float32
PIECES = 4
DIRECT_SCATTER = (0,)
DIRECT_GATHER = (0, 3)
Z_FIRST = (1,)
EXCHANGE_VMEM = 40 * 1024 * 1024
FINISH_VMEM = 24 * 1024 * 1024


def permutation(inner_bits):
    outer_bits = 8 - inner_bits
    at = lax.broadcasted_iota(jnp.int32, (256, 256), 0)
    of = lax.broadcasted_iota(jnp.int32, (256, 256), 1)
    want = ((at & ((1 << outer_bits) - 1)) << inner_bits) + (at >> outer_bits)
    return jnp.where(of == want, 1.0, 0.0).astype(BF)


def side_by_side(blocks):
    return jnp.concatenate([jnp.concatenate(rows, axis=0) for rows in blocks], axis=1)


def spread_states(perm, values, store):
    for h in range(values.shape[0] // 64):
        stack = side_by_side(
            [
                [
                    values[(2 * h + k) * 32:(2 * h + k + 1) * 32, b * 256 + jt * 128:b * 256 + (jt + 1) * 128]
                    for jt in range(2) for b in range(4)
                ]
                for k in range(2)
            ]
        )
        turned = jnp.dot(perm, stack, preferred_element_type=F32).astype(BF)
        for k in range(2):
            store(2 * h + k, turned[:, k * 128:(k + 1) * 128])


def four_states(parts):
    last = -(parts[0].astype(F32) + parts[1].astype(F32) + parts[2].astype(F32))
    return list(parts) + [last.astype(BF)]


def piece_rows(rg):
    return four_states(
        [
            jnp.concatenate([rg[xc, :, a].reshape(128, 128) for xc in range(4)], axis=1)
            for a in range(3)
        ]
    )


def onehot(states, value):
    return jnp.where(states == value, 1.0, 0.0).astype(BF)


def piece_gradient(parts, heads, rhs, right_sum):
    lhs = jnp.concatenate(
        [jnp.concatenate([parts[a], heads[a]], axis=1) for a in range(3)], axis=0
    )
    nine = jnp.dot(lhs, rhs[:, pl.ds(0, 768)], preferred_element_type=F32)
    sums = [jnp.sum(parts[a].astype(F32), axis=1, keepdims=True) for a in range(3)]
    blocks = []
    for a in range(3):
        row = [nine[a * 128:(a + 1) * 128, b * 256:(b + 1) * 256] for b in range(3)]
        blocks.append(row + [-sums[a] - (row[0] + row[1] + row[2])])
    last = [
        right_sum[pl.ds(0, 1), pl.ds(b * 256, 256)] - (blocks[0][b] + blocks[1][b] + blocks[2][b])
        for b in range(3)
    ]
    blocks.append(last + [(sums[0] + sums[1] + sums[2]) - (last[0] + last[1] + last[2])])
    return [jnp.concatenate([block.astype(BF) for block in row], axis=1) for row in blocks]


def softmax_residual(diffs, states):
    top = jnp.maximum(jnp.maximum(diffs[0], diffs[1]), jnp.maximum(diffs[2], 0.0))
    exps = [jnp.exp(d - top) for d in diffs]
    inverse = 1.0 / (exps[0] + exps[1] + exps[2] + jnp.exp(-top))
    return [
        (jnp.where(states == a, 1.0, 0.0) - exps[a] * inverse).astype(BF) for a in range(3)
    ]


def exchange_kernel(
    left_in, right_in, lbias_in, rbias_in, coup_ref,
    grad_out, nat_out, rres_out, rhs_out, rg_out, lht_out,
    left_ref, right_ref, lbias_ref, rbias_ref, raw, flat, perm, spread, grads, nat, rres, rhs, rsum, lht, rt, loh, slt, bt,
    lp, xa, xb, zp, zb, rg,
    cs, cr, own, yp, yb, tz, zs, zr, rr,
    in_sem, out_sem, lsend, lrecv, rsend, rrecv,
):
    row = lax.axis_index("row")
    col = lax.axis_index("col")
    core = lax.rem(row, 2)
    zl = lax.rem(lax.div(row, 2), 2)
    y = lax.div(row, 4)
    x = lax.div(col, 4)
    z = lax.rem(col, 4)

    def at_x(d):
        return {"row": row, "col": lax.rem(x + d, 4) * 4 + z}

    def at_z(d):
        return {"row": row, "col": x * 4 + lax.rem(z + d, 4)}

    def at_y(d):
        return {"row": lax.rem(y + d, 4) * 4 + zl * 2 + core, "col": col}

    core_peer = {"row": y * 4 + zl * 2 + 1 - core, "col": col}
    zl_peer = {"row": y * 4 + (1 - zl) * 2 + core, "col": col}
    peers = [at(d) for at in (at_x, at_z, at_y) for d in (1, 2, 3)] + [zl_peer, core_peer]

    def axes(p):
        return ((z, at_z), (x, at_x)) if p in Z_FIRST else ((x, at_x), (z, at_z))

    def chunk(ref, p, index, part=pl.ds(0, 4)):
        return ref.at[p, part, index] if p in Z_FIRST else ref.at[p, index, part]

    low, high = pl.ds(0, 2), pl.ds(2, 2)

    barrier = pltpu.get_barrier_semaphore()
    for peer in peers:
        pl.semaphore_signal(barrier, inc=1, device_id=peer, device_id_type=MESH)

    loads = {}

    def load(key, src, dst):
        copy = pltpu.make_async_copy(src, dst, in_sem.at[len(loads)])
        copy.start()
        loads[key] = copy

    load("right", right_in, right_ref)
    for p in range(PIECES):
        rows = pl.ds(p * 1024, 1024)
        load(p, coup_ref.at[:, rows, :], raw.at[:, rows, :])
        if p == 0:
            load("left", left_in, left_ref)
            load("lbias", lbias_in, lbias_ref)
            load("rbias", rbias_in, rbias_ref)

    sent = []

    def send(src, dst, sems, slot, peer):
        copy = pltpu.make_async_remote_copy(
            src_ref=src, dst_ref=dst, send_sem=sems[0].at[slot], recv_sem=sems[1].at[slot],
            device_id=peer, device_id_type=MESH,
        )
        copy.start()
        sent.append(copy)
        return copy

    lsems = (lsend, lrecv)
    rsems = (rsend, rrecv)

    perm[...] = permutation(3)
    spread[...] = permutation(5)
    loads["right"].wait()
    right_t = right_ref[...].T
    for b in range(4):
        rt[pl.ds(b * 256, 256), :] = onehot(right_t, b)

    live = {}

    def left_fields(p):
        loads[p].wait()
        for a in range(4):
            for h in range(2):
                pair = [
                    raw[a, pl.ds(p * 1024 + (2 * h + k) * 256, 256), :] for k in range(2)
                ]
                turned = jnp.dot(
                    perm[...], jnp.concatenate(pair, axis=1), preferred_element_type=F32
                ).astype(BF)
                for k in range(2):
                    for jt in range(2):
                        for b in range(4):
                            flat[
                                pl.ds(a * 512 + p * 128 + (2 * h + k) * 32, 32),
                                pl.ds(b * 256 + jt * 128, 128),
                            ] = turned[(jt * 4 + b) * 32:(jt * 4 + b + 1) * 32, k * 128:(k + 1) * 128]
        lhs = jnp.concatenate([flat[pl.ds(a * 512 + p * 128, 128), :] for a in range(4)], axis=0)
        fields = jnp.dot(lhs, rt[...], preferred_element_type=F32)
        for a in range(3):
            diff = (fields[a * 128:(a + 1) * 128] - fields[384:512]).astype(BF)
            for xc in range(4):
                for zc in range(4):
                    lp[p, xc, zc, a] = diff[zc * 32:(zc + 1) * 32, xc * 128:(xc + 1) * 128]

    def first_scatter(p):
        me, at = axes(p)[0]
        if p in DIRECT_SCATTER:
            for d in (2, 1, 3):
                live[p, d] = send(chunk(lp, p, lax.rem(me + d, 4)), xb.at[p, d - 1], lsems, p * 16 + d, at(d))
            return
        opp, nxt, prv = lax.rem(me + 2, 4), lax.rem(me + 1, 4), lax.rem(me + 3, 4)
        live[p, 0] = send(chunk(lp, p, opp, low), xa.at[p, 0], lsems, p * 16 + 0, at(1))
        live[p, 1] = send(chunk(lp, p, opp, high), xa.at[p, 1], lsems, p * 16 + 1, at(3))
        live[p, 2] = send(chunk(lp, p, nxt, high), xb.at[p, 0, high], lsems, p * 16 + 2, at(1))
        live[p, 3] = send(chunk(lp, p, prv, low), xb.at[p, 1, low], lsems, p * 16 + 3, at(3))

    def relay(p):
        me, at = axes(p)[0]
        mine = chunk(lp, p, lax.rem(me + 1, 4), low)
        live[p, 0].wait_recv()
        mine[...] = (mine[...].astype(F32) + xa[p, 0].astype(F32)).astype(BF)
        live[p, 4] = send(mine, xb.at[p, 0, low], lsems, p * 16 + 4, at(1))
        mine = chunk(lp, p, lax.rem(me + 3, 4), high)
        live[p, 1].wait_recv()
        mine[...] = (mine[...].astype(F32) + xa[p, 1].astype(F32)).astype(BF)
        live[p, 5] = send(mine, xb.at[p, 1, high], lsems, p * 16 + 5, at(3))

    def second_scatter(p):
        (first, _), (me, at) = axes(p)
        direct = p in DIRECT_SCATTER
        for m in (1, 2, 3) if direct else (2, 3, 4, 5):
            live[p, m].wait_recv()
        total = chunk(lp, p, first)[...].astype(F32) + xb[p, 0].astype(F32) + xb[p, 1].astype(F32)
        if direct:
            total = total + xb[p, 2].astype(F32)
        zp[p] = total.astype(BF)
        for d in (2, 1, 3):
            live[p, 5 + d] = send(zp.at[p, lax.rem(me + d, 4)], zb.at[p, d - 1], lsems, p * 16 + 5 + d, at(d))

    def first_gather(p):
        me, at = axes(p)[1]
        for m in (6, 7, 8):
            live[p, m].wait_recv()
        total = zp[p, me].astype(F32)
        for k in range(3):
            total = total + zb[p, k].astype(F32)
        rows = pl.ds(pl.multiple_of(p * 128 + z * 32, 32), 32)
        diffs = [total[a] + bt[a, rows, :] for a in range(3)]
        result = softmax_residual(diffs, slt[x, rows, :])
        for a in range(3):
            rg[p, x, z, a] = result[a]
        block = rg.at[p, x, z]
        for d in (2, 1, 3):
            live[p, 8 + d] = send(block, block, lsems, p * 16 + 8 + d, at(d))

    def second_gather(p):
        me, at = axes(p)[0]
        for m in (9, 10, 11):
            live[p, m].wait_recv()
        block = chunk(rg, p, me)
        for d in (2, 1, 3) if p in DIRECT_GATHER else (1, 3):
            live[p, 11 + d] = send(block, block, lsems, p * 16 + 11 + d, at(d))

    def forward(p):
        me, at = axes(p)[0]
        live[p, 12].wait_recv()
        block = chunk(rg, p, lax.rem(me + 3, 4), low)
        live[p, 13] = send(block, block, lsems, p * 16 + 13, at(1))
        live[p, 14].wait_recv()
        block = chunk(rg, p, lax.rem(me + 1, 4), high)
        live[p, 15] = send(block, block, lsems, p * 16 + 15, at(3))

    finals = []

    def keep(src, dst):
        copy = pltpu.make_async_copy(src, dst, out_sem.at[len(finals)])
        copy.start()
        finals.append(copy)

    def left_done(p):
        for m in (12, 13, 14) if p in DIRECT_GATHER else (13, 15):
            live[p, m].wait_recv()
        if p == PIECES - 1:
            keep(rg.at[p], rg_out)

    def gradient_piece(p):
        parts = piece_rows(rg[p])
        for a in range(4):
            turned = parts[a].astype(F32).T.astype(BF)
            nat[p * 4 + a] = turned
        keep(nat.at[pl.ds(p * 4, 4)], nat_out.at[pl.ds(p * 4, 4)])
        heads = [lht[a, pl.ds(p * 128, 128), :] for a in range(3)]
        for a, values in enumerate(piece_gradient(parts, heads, rhs, rsum)):

            def store(block, rows):
                grads[a, pl.ds(p * 1024 + block * 256, 256), :] = rows

            spread_states(spread[...], values, store)
        rows = pl.ds(p * 1024, 1024)
        keep(grads.at[:, rows, :], grad_out.at[:, rows, :])

    def right_diffs(half):
        lhs = loh[pl.ds(pl.multiple_of(half * 256, 256), 256), :]
        fields = jnp.dot(lhs, flat[...], preferred_element_type=F32)
        return [fields[:, b * 256:(b + 1) * 256] - fields[:, 768:1024] for b in range(3)]

    def core_scatter():
        for b, diff in enumerate(right_diffs(1 - core)):
            cs[:, pl.ds(b * 256, 256)] = diff.astype(BF)
        live["c"] = send(cs, cr, rsems, 0, core_peer)

    def right_own():
        for b, diff in enumerate(right_diffs(core)):
            own[:, pl.ds(b * 256, 256)] = diff

    def y_scatter():
        live["c"].wait_recv()
        for c in range(4):
            rows = pl.ds(c * 64, 64)
            yp[c] = (own[rows, :] + cr[rows, :].astype(F32)).astype(BF)
        for d in (2, 1, 3):
            live["ys", d] = send(yp.at[lax.rem(y + d, 4)], yb.at[d - 1], rsems, d, at_y(d))

    def zl_scatter():
        for d in (1, 2, 3):
            live["ys", d].wait_recv()
        total = yp[y].astype(F32)
        for k in range(3):
            total = total + yb[k].astype(F32)
        tz[0] = total[:32]
        tz[1] = total[32:]
        zs[...] = tz[1 - zl].astype(BF)
        live["zs"] = send(zs, zr, rsems, 4, zl_peer)

    def right_rows(start, count):
        return pl.ds(pl.multiple_of(start, 32), count)

    def zl_gather():
        live["zs"].wait_recv()
        total = tz[zl] + zr[...].astype(F32)
        rows = right_rows(core * 256 + y * 64 + zl * 32, 32)
        base = rbias_ref[pl.ds(3, 1), :]
        diffs = [
            total[:, b * 256:(b + 1) * 256] + (rbias_ref[pl.ds(b, 1), :] - base) for b in range(3)
        ]
        for b, part in enumerate(softmax_residual(diffs, right_ref[rows, :])):
            rr[rows, pl.ds(b * 256, 256)] = part
        block = rr.at[rows, :]
        live["zg"] = send(block, block, rsems, 5, zl_peer)

    def y_gather():
        live["zg"].wait_recv()
        block = rr.at[right_rows(core * 256 + y * 64, 64), :]
        for d in (2, 1, 3):
            live["yg", d] = send(block, block, rsems, 5 + d, at_y(d))

    def core_gather():
        for d in (1, 2, 3):
            live["yg", d].wait_recv()
        block = rr.at[right_rows(core * 256, 256), :]
        live["c1"] = send(block, block, rsems, 9, core_peer)

    def right_done():
        live["c1"].wait_recv()
        parts = four_states([rr[:, pl.ds(b * 256, 256)] for b in range(3)])
        for b in range(4):
            rhs[pl.ds(512, 512), pl.ds(b * 256, 256)] = -parts[b]
        for b in range(3):
            total = jnp.sum(-parts[b].astype(F32), axis=0, keepdims=True)
            rsum[:, pl.ds(b * 256, 256)] = jnp.broadcast_to(total, (8, 256))
        keep(rhs, rhs_out)

    def right_spread():
        def store(block, rows):
            rres[pl.ds(block * 256, 256), :] = rows

        spread_states(spread[...], -rhs[pl.ds(512, 512), :], store)
        keep(rres, rres_out)

    def right_onehots():
        states = right_ref[...]
        for b in range(4):
            rhs[pl.ds(0, 512), pl.ds(b * 256, 256)] = -onehot(states, b)

    def left_tables():
        left_t = left_ref[...].T
        for xc in range(4):
            slt[xc] = left_t[:, xc * 128:(xc + 1) * 128]
        for a in range(4):
            lht[a] = onehot(left_t, a)
        keep(lht.at[:, pl.ds((PIECES - 1) * 128, 128), :], lht_out)
        base = lbias_ref[pl.ds(3, 1), :]
        for a in range(3):
            diff = lbias_ref[pl.ds(a, 1), :] - base
            for p in range(PIECES):
                part = jnp.broadcast_to(diff[:, p * 128:(p + 1) * 128], (128, 128))
                bt[a, pl.ds(p * 128, 128), :] = part.T

    def left_onehots():
        states = left_ref[...]
        for a in range(4):
            loh[:, pl.ds(a * 512, 512)] = onehot(states, a)

    left_fields(0)
    pl.semaphore_wait(barrier, len(peers))
    first_scatter(0)
    left_fields(1)
    first_scatter(1)
    left_fields(2)
    first_scatter(2)
    left_fields(3)
    for key in ("left", "lbias", "rbias"):
        loads[key].wait()
    left_onehots()
    core_scatter()
    first_scatter(3)
    second_scatter(0)
    right_own()
    relay(2)
    y_scatter()
    relay(1)
    second_scatter(2)
    left_tables()
    first_gather(0)
    relay(3)
    second_scatter(1)
    zl_scatter()
    first_gather(2)
    first_gather(1)
    zl_gather()
    second_gather(0)
    second_scatter(3)
    second_gather(1)
    second_gather(2)
    y_gather()
    right_onehots()
    first_gather(3)
    forward(2)
    core_gather()
    forward(1)
    second_gather(3)
    left_done(0)
    left_done(2)
    right_done()
    gradient_piece(2)
    right_spread()
    left_done(1)
    gradient_piece(1)
    gradient_piece(0)
    left_done(3)
    for copy in sent:
        copy.wait_send()
    for copy in finals:
        copy.wait()


def exchange(left_states, right_states, left_bias, right_bias, couplings):
    hbm = pl.BlockSpec(memory_space=pltpu.HBM)
    any_space = pl.BlockSpec(memory_space=pl.ANY)
    n = PIECES
    return pl.pallas_call(
        exchange_kernel,
        out_shape=(
            jax.ShapeDtypeStruct((4, 3072, 128), BF),
            jax.ShapeDtypeStruct((12, 512, 128), BF),
            jax.ShapeDtypeStruct((4096, 128), BF),
            jax.ShapeDtypeStruct((1024, 1024), BF),
            jax.ShapeDtypeStruct((4, 4, 3, 32, 128), BF),
            jax.ShapeDtypeStruct((4, 128, 512), BF),
        ),
        in_specs=[hbm] * 5,
        out_specs=(any_space,) * 6,
        scratch_shapes=[
            pltpu.VMEM((512, 512), jnp.int32),
            pltpu.VMEM((512, 256), jnp.int32),
            pltpu.VMEM((4, 512), F32),
            pltpu.VMEM((4, 256), F32),
            pltpu.VMEM((4, 4096, 128), BF),
            pltpu.VMEM((2048, 1024), BF),
            pltpu.VMEM((256, 256), BF),
            pltpu.VMEM((256, 256), BF),
            pltpu.VMEM((4, 3072, 128), BF),
            pltpu.VMEM((12, 512, 128), BF),
            pltpu.VMEM((4096, 128), BF),
            pltpu.VMEM((1024, 1024), BF),
            pltpu.VMEM((8, 768), F32),
            pltpu.VMEM((4, 512, 512), BF),
            pltpu.VMEM((1024, 512), BF),
            pltpu.VMEM((512, 2048), BF),
            pltpu.VMEM((4, 512, 128), jnp.int32),
            pltpu.VMEM((3, 512, 128), F32),
            pltpu.VMEM((n, 4, 4, 3, 32, 128), BF),
            pltpu.VMEM((n, 2, 2, 3, 32, 128), BF),
            pltpu.VMEM((n, 3, 4, 3, 32, 128), BF),
            pltpu.VMEM((n, 4, 3, 32, 128), BF),
            pltpu.VMEM((n, 3, 3, 32, 128), BF),
            pltpu.VMEM((n, 4, 4, 3, 32, 128), BF),
            pltpu.VMEM((256, 768), BF),
            pltpu.VMEM((256, 768), BF),
            pltpu.VMEM((256, 768), F32),
            pltpu.VMEM((4, 64, 768), BF),
            pltpu.VMEM((3, 64, 768), BF),
            pltpu.VMEM((2, 32, 768), F32),
            pltpu.VMEM((32, 768), BF),
            pltpu.VMEM((32, 768), BF),
            pltpu.VMEM((512, 768), BF),
            pltpu.SemaphoreType.DMA((n + 4,)),
            pltpu.SemaphoreType.DMA((10,)),
            pltpu.SemaphoreType.DMA((n * 16,)),
            pltpu.SemaphoreType.DMA((n * 16,)),
            pltpu.SemaphoreType.DMA((10,)),
            pltpu.SemaphoreType.DMA((10,)),
        ],
        compiler_params=pltpu.CompilerParams(
            collective_id=0, has_side_effects=True, vmem_limit_bytes=EXCHANGE_VMEM
        ),
        name="exchange",
    )(*[pltpu.with_memory_space_constraint(v, pltpu.HBM) for v in (left_states, right_states, left_bias, right_bias, couplings)])


def finish_kernel(
    part_ref, nat_ref, rres_ref, rhs_ref, rg_ref, lht_ref,
    lres_out, rres_out, grad_out,
    grads, lres, sems,
):
    copies = []

    def put(src, dst):
        copy = pltpu.make_async_copy(src, dst, sems.at[len(copies)])
        copy.start()
        copies.append(copy)

    put(part_ref, grad_out.at[:, pl.ds(0, 3072), :])
    put(rres_ref, rres_out)
    spread = permutation(5)
    gather = permutation(4)
    parts = piece_rows(rg_ref[...])

    def last_piece(h):
        lhs = jnp.concatenate(
            [jnp.concatenate([parts[a], lht_ref[a]], axis=1) for a in (2 * h, 2 * h + 1)], axis=0
        )
        summed = jnp.dot(lhs, rhs_ref[...], preferred_element_type=F32).astype(BF)
        for k in range(2):
            a = 2 * h + k

            def store(block, rows):
                grads[a, pl.ds(block * 256, 256), :] = rows

            spread_states(spread, summed[k * 128:(k + 1) * 128], store)
        states = pl.ds(2 * h, 2)
        put(grads.at[states], grad_out.at[states, pl.ds(3072, 1024), :])

    last_piece(0)
    turned = [part.astype(F32).T.astype(BF) for part in parts]
    for q in range(4):
        for h in range(4 * q, 4 * q + 4):
            stack = side_by_side(
                [
                    [nat_ref[m, pl.ds((2 * h + k) * 16, 16), :] for m in range(12)]
                    + [block[(2 * h + k) * 16:(2 * h + k + 1) * 16] for block in turned]
                    for k in range(2)
                ]
            )
            rows = jnp.dot(gather, stack, preferred_element_type=F32).astype(BF)
            for k in range(2):
                lres[pl.ds((2 * h + k) * 256, 256), :] = rows[:, k * 128:(k + 1) * 128]
        block = pl.ds(q * 2048, 2048)
        put(lres.at[block, :], lres_out.at[block, :])
    last_piece(1)
    for copy in copies:
        copy.wait()


def finish(part, nat, rres, rhs, rg, lht):
    vmem = pl.BlockSpec(memory_space=pltpu.VMEM)
    any_space = pl.BlockSpec(memory_space=pl.ANY)
    return pl.pallas_call(
        finish_kernel,
        out_shape=(
            jax.ShapeDtypeStruct((8192, 128), BF),
            jax.ShapeDtypeStruct((4096, 128), BF),
            jax.ShapeDtypeStruct((4, 4096, 128), BF),
        ),
        in_specs=[any_space, vmem, any_space, vmem, vmem, vmem],
        out_specs=(pl.BlockSpec(memory_space=pltpu.HBM),) * 3,
        scratch_shapes=[
            pltpu.VMEM((4, 1024, 128), BF),
            pltpu.VMEM((8192, 128), BF),
            pltpu.SemaphoreType.DMA((8,)),
        ],
        compiler_params=pltpu.CompilerParams(vmem_limit_bytes=FINISH_VMEM),
        name="finish",
    )(part, nat, rres, rhs, rg, lht)


def body(left_states, right_states, left_bias, right_bias, couplings):
    view = couplings.reshape(4, 512, 4, 2, 128).transpose(0, 1, 3, 2, 4).reshape(4, 4096, 128)
    kept = exchange(left_states, right_states, left_bias, right_bias, view)
    left, right, grad = finish(*kept)
    left_residual = left.reshape(512, 4, 4, 128).transpose(0, 2, 1, 3).reshape(512, 4, 512)
    right_residual = right.reshape(512, 2, 4, 128).transpose(0, 2, 1, 3).reshape(512, 4, 256)
    coupling_grad = grad.reshape(4, 512, 2, 4, 128).transpose(0, 1, 3, 2, 4).reshape(4, 512, 4, 256)
    return left_residual, right_residual, coupling_grad


def solution(mesh):
    in_specs = (
        P(None, "row"),
        P(None, "col"),
        P(None, "row"),
        P(None, "col"),
        P(None, "row", None, "col"),
    )
    out_specs = (P(None, None, "row"), P(None, None, "col"), P(None, "row", None, "col"))
    return jax.shard_map(body, mesh=mesh, in_specs=in_specs, out_specs=out_specs, check_vma=False)
```
